256 devices in a mesh: seq: 32 (over z_lo, y, core), head: 8 (over z_hi, x).
Axes of the slice: x: 4, y: 4, z: 8 (z_hi: 2, z_lo: 4; z = z_hi * 4 + z_lo), core: 2. Of those that a mesh axis runs over, the one named last changes fastest.
Arguments:
- queries: bfloat16 [4096, 8192], P('seq', 'head'), may hold values from -30 to 30
- cache: bfloat16 [16384, 2048], P('seq', 'head'), may hold values from -30 to 30
- stretch_kv: bfloat16 [4096, 2048], P(('seq', 'head')), may hold values from -6 to 6
- stretch_pos: int32 [32], replicated, may hold values from 0 to 31, each once
Outputs:
- attended: bfloat16 [4096, 8192], P('seq', 'head')
The draws below stay inside these ranges and needn't reach their ends.
Inputs may be any that keep to these rules, and one draw needn't show every extreme that they name: `stretch_pos`: each block position appears once.
All inputs are finite; a program needn't handle non-finite values.
Results may differ from the reference program's by a relative error of at most 0.012.
Values may be sent and summed in bfloat16 or wider, within the bound.
A program may use at most 192 MiB of HBM per device.

```python
import math
import jax
import jax.numpy as jnp
from jax import lax

HQ = 64
KVH = 8
HD = 128
QD = 128
CTX = 16384
QTOK = 4096
N_SEQ = 32


def draw_queries(key, part):
    key = jax.random.fold_in(key, 11)
    first, second = jax.random.split(key)
    base = (jax.random.randint(first, (QTOK, HQ * HD), -48, 49) + jax.random.randint(second, (QTOK, HQ * HD), -48, 49)).astype(jnp.float32) / 32.0
    return base.astype(jnp.bfloat16)


def draw_cache(key, part):
    key = jax.random.fold_in(key, 23)
    first, second = jax.random.split(key)
    base = (jax.random.randint(first, (CTX, KVH, 2, HD), -48, 49) + jax.random.randint(second, (CTX, KVH, 2, HD), -48, 49)).astype(jnp.float32) / 32.0
    return base.reshape(CTX, KVH * 2 * HD).astype(jnp.bfloat16)


def draw_stretch_kv(key, part):
    key = jax.random.fold_in(key, 37)
    first, second = jax.random.split(key)
    base = (jax.random.randint(first, (QTOK, KVH * 2 * HD), -48, 49) + jax.random.randint(second, (QTOK, KVH * 2 * HD), -48, 49)).astype(jnp.float32) / 32.0
    return base.astype(jnp.bfloat16)


def setup_inputs(seed: int = 0) -> dict:
    arg_keys = jax.random.split(jax.random.key(seed), 5)
    queries = draw_queries(jax.random.fold_in(arg_keys[4], 71), 0)
    cache = draw_cache(jax.random.fold_in(arg_keys[4], 71), 0)
    stretch_kv = draw_stretch_kv(jax.random.fold_in(arg_keys[4], 71), 0)
    stretch_pos = jax.random.permutation(arg_keys[3], N_SEQ).astype(jnp.int32)
    return {"queries": queries, "cache": cache, "stretch_kv": stretch_kv, "stretch_pos": stretch_pos}


def reference(queries, cache, stretch_kv, stretch_pos):
    group = HQ // KVH
    block = math.gcd(QTOK, 512)
    rows = jnp.arange(QTOK, dtype=jnp.int32)
    qpos = stretch_pos[rows // QD] * QD + rows % QD
    kv_all = jnp.concatenate([cache, stretch_kv], 0).reshape(CTX + QTOK, KVH, 2, HD)
    kpos = jnp.concatenate([jnp.full((CTX,), -1, jnp.int32), qpos.astype(jnp.int32)])
    qall = queries.reshape(QTOK // block, block, KVH, group, HD)
    pall = qpos.reshape(QTOK // block, block)

    def per_head(head):
        keys = kv_all[:, head, 0].astype(jnp.float32)
        values = kv_all[:, head, 1].astype(jnp.float32)

        def one_block(args):
            qb, pb = args
            qh = qb[:, head].astype(jnp.float32)
            scores = jnp.einsum("rgd,cd->grc", qh, keys) * (HD ** -0.5)
            scores = jnp.where(kpos[None, None, :] <= pb[None, :, None], scores, -1e30)
            top = jnp.max(scores, -1, keepdims=True)
            expo = jnp.exp(scores - top)
            total = jnp.sum(expo, -1)
            probs = expo.astype(jnp.bfloat16).astype(jnp.float32)
            outp = jnp.einsum("grc,cd->rgd", probs, values) / jnp.transpose(total)[:, :, None]
            return outp

        return lax.map(one_block, (qall, pall))

    heads = lax.map(per_head, jnp.arange(KVH, dtype=jnp.int32))
    out = jnp.transpose(heads, (1, 2, 0, 3, 4)).reshape(QTOK, HQ * HD)
    return out.astype(jnp.bfloat16)
```

```python
import functools

import jax
import jax.numpy as jnp
from jax import lax
from jax.experimental import pallas as pl
from jax.experimental.pallas import tpu as pltpu
from jax.sharding import PartitionSpec as P

MESH = pl.DeviceIdType.MESH
F32, BF16 = jnp.float32, jnp.bfloat16
HD = 128
QD = 128
CHUNK = 1024
PIECE = 512
TILE = 256
BIG = 1e30
UNITS = (
    (0, 0), (1, 0), (0, 1), (1, 1), (2, 0), (2, 1), (3, 1), (3, 0), (4, 1), (4, 0),
    (8, 1), (5, 1), (5, 0), (6, 1), (9, 1), (7, 1), (8, 0), (6, 0), (9, 0), (7, 0),
)
LAST_PARTNER = max(u for u, (_, owner) in enumerate(UNITS) if owner == 1)


def fold(x, op):
    parts = [x[8 * i : 8 * i + 8] for i in range(x.shape[0] // 8)]
    while len(parts) > 1:
        parts = [op(a, b) for a, b in zip(parts[::2], parts[1::2])]
    return parts[0]


def dot(a, b):
    return lax.dot_general(a, b, (((1,), (0,)), ((), ())), preferred_element_type=F32)


def lookup(u, values):
    found = jnp.int32(values[0])
    for k, value in enumerate(values):
        if k and value != 0:
            found = jnp.where(u == k, jnp.int32(value), found)
        elif k and values[0] != 0:
            found = jnp.where(u == k, jnp.int32(0), found)
    return found


def region(kv, slot, half, lane):
    if slot in (0, 7):
        return kv.at[slot, pl.ds(lane * 512 + half * 256, 256)]
    chunk = 2 * ((slot + 1) // 2) - 1 + half
    return kv.at[chunk, pl.ds((0 if slot % 2 else 512) + lane * 256, 256)]


def new_pair(kv, d, lane):
    return kv.at[8 + d // 2, pl.ds((d % 2) * 512 + lane * 256, 256)]


def kernel(
    q_ref, cache_ref, new_ref, pos_ref, out_ref,
    kv, vt, qt, q_in, scores, acc, top, total, tri, bias, po, plse, so, slse,
    lane_r, sib_r, yk_s, sib_s, z1_s, z3_s, all_s, all_r, loc, ny_s, ny_r, nz_r, nz1_s, nz3_s, nsib_s, nsib_r,
    q_s, q_r, o_s, o_r,
):
    me = lax.axis_index("seq")
    head = lax.axis_index("head")
    heads = 8
    core = me % 2
    y = (me // 2) % 4
    z = me // 8

    def at(zz, yy, cc):
        return {"seq": (zz * 4 + yy) * 2 + cc}

    yk = y + 1 - 2 * (y % 2)
    yp = 3 - y
    z1 = z + 1 - 2 * (z % 2)
    z2 = (z + 2) % 4
    z3 = 3 - z
    oc = 1 - core
    mid = jnp.logical_or(z == 1, z == 2)
    end = jnp.logical_or(z == 0, z == 3)
    to_sib, to_yk, to_z1, to_z3, to_p = at(z, y, oc), at(z, yk, core), at(z1, y, core), at(z3, y, core), at(z, yp, core)

    def remote(src, dst, ss, rs, dev):
        return pltpu.make_async_remote_copy(
            src_ref=src, dst_ref=dst, send_sem=ss, recv_sem=rs, device_id=dev, device_id_type=MESH
        )

    def sib(slot, h):
        src = cache_ref.at[pl.ds(h * 256, 256)] if slot == 0 else region(kv, slot, h, 0)
        return remote(src, region(kv, slot, h, 1), sib_s.at[slot, h], sib_r.at[slot, h], to_sib)

    def ykm(d, h):
        src = cache_ref.at[pl.ds(h * 256, 256)] if d == 0 else region(kv, 2 * d, h, 0)
        return remote(src, region(kv, 2 * d + 1, h, 0), yk_s.at[d, h], lane_r.at[2 * d + 1, h], to_yk)

    def z1m(d, h):
        src = cache_ref.at[pl.ds(h * 256, 256)] if d == 1 else region(kv, 6 if d == 2 else 4, h, 0)
        return remote(src, region(kv, 2 * d, h, 0), z1_s.at[d, h], lane_r.at[2 * d, h], to_z1)

    def z3m(d, h):
        src = cache_ref.at[pl.ds(h * 256, 256)] if d == 3 else region(kv, 2, h, 0)
        return remote(src, region(kv, 2 * d, h, 0), z3_s.at[d, h], lane_r.at[2 * d, h], to_z3)

    def spread(k):
        g = (head + k) % heads
        return remote(
            new_ref.at[:, pl.ds(pl.multiple_of(g * 256, 256), 256)],
            kv.at[8, pl.ds(pl.multiple_of(head * 16, 16), 16)],
            all_s.at[k], all_r.at[k], {"head": g},
        )

    def spread_in(k):
        g = (head + heads - k) % heads
        spot = kv.at[8, pl.ds(pl.multiple_of(g * 16, 16), 16)]
        return remote(spot, spot, all_s.at[k], all_r.at[k], {"head": g})

    def own_new():
        return pltpu.make_async_copy(
            new_ref.at[:, pl.ds(pl.multiple_of(head * 256, 256), 256)],
            kv.at[8, pl.ds(pl.multiple_of(head * 16, 16), 16)],
            loc.at[0],
        )

    def ny():
        return remote(kv.at[8, pl.ds(0, 128)], kv.at[8, pl.ds(128, 128)], ny_s.at[0], ny_r.at[0], to_yk)

    def nsib(d):
        return remote(new_pair(kv, d, 0), new_pair(kv, d, 1), nsib_s.at[d], nsib_r.at[d], to_sib)

    def nz1(d):
        return remote(new_pair(kv, (0, 0, 3, 2)[d], 0), new_pair(kv, d, 0), nz1_s.at[d], nz_r.at[d], to_z1)

    def nz3(d):
        return remote(new_pair(kv, 0 if d == 3 else 1, 0), new_pair(kv, d, 0), nz3_s.at[d], nz_r.at[d], to_z3)

    def qm(h):
        cols = pl.ds(h * 512, 512)
        return remote(q_ref.at[:, cols], q_in.at[:, cols], q_s.at[h], q_r.at[h], to_p)

    def om(t):
        return remote(so.at[t], po.at[t], o_s.at[t, 0], o_r.at[t, 0], to_p)

    def lm(t):
        return remote(slse.at[t], plse.at[t], o_s.at[t, 1], o_r.at[t, 1], to_p)

    barrier = pltpu.get_barrier_semaphore()
    peers = [to_sib, to_yk, to_z1, to_z3, to_p] + [{"head": (head + k) % heads} for k in range(1, heads)]
    for peer in peers:
        pl.semaphore_signal(barrier, inc=1, device_id=peer, device_id_type=MESH)

    kv[0, :512, :] = cache_ref[...]
    key_at = lax.broadcasted_iota(jnp.int32, (QD, TILE), 0)
    row_at = lax.broadcasted_iota(jnp.int32, (QD, TILE), 1) % QD
    tri[0] = jnp.zeros((QD, TILE), F32)
    tri[1] = jnp.where(key_at <= row_at, 0.0, -BIG)
    for owner in range(2):
        row_pos = pos_ref[me if owner == 0 else (z * 4 + yp) * 2 + core]
        for b in range(8):
            bias[owner * 8 + b] = jnp.float32(0.0)
        for b in range(16):
            d, lane, yr = b // 4, (b // 2) % 2, b % 2
            zz = (z, z1, z2, z3)[d]
            seq = (zz * 4 + (yk if yr else y)) * 2 + (oc if lane else core)
            if owner == 0 and b == 0:
                hidden = jnp.float32(0.0)
            else:
                hidden = jnp.where(pos_ref[seq] < row_pos, 0.0, BIG).astype(F32)
            bias[((1 + b // 8) * 2 + owner) * 8 + b % 8] = hidden
    acc[...] = jnp.zeros_like(acc)
    top[...] = jnp.full_like(top, -BIG)
    total[...] = jnp.zeros_like(total)

    def place_queries(ref, owner):
        for h in range(8):
            q = ref[:, h * HD : (h + 1) * HD].astype(F32) * (HD ** -0.5 * 1.4426950408889634)
            high = q.astype(BF16)
            low = (q - high.astype(F32)).astype(BF16)
            cols = pl.ds(owner * 1024 + h * HD, HD)
            qt[:HD, cols] = high.T
            qt[HD:, cols] = low.T

    place_queries(q_ref, 0)

    pl.semaphore_wait(barrier, len(peers))

    own_new().start()
    for h in range(2):
        qm(h).start()
        ykm(0, h).start()
        z1m(1, h).start()

        @pl.when(mid)
        def _():
            z3m(3, h).start()

        sib(0, h).start()
        if h == 0:
            for k in range(1, heads):
                spread(k).start()

    def from_yk(slot, h):
        ykm(slot // 2, h).wait_recv()
        sib(slot, h).start()

    def first_line(h):
        z1m(1, h).wait_recv()
        ykm(1, h).start()
        sib(2, h).start()

        @pl.when(mid)
        def _():
            z3m(2, h).start()
            z3m(3, h).wait_recv()
            z1m(2, h).start()

        from_yk(1, h)

    def second_line(h):
        z1m(2, h).wait_recv()
        ykm(2, h).start()
        sib(4, h).start()

        @pl.when(mid)
        def _():
            z1m(3, h).start()

        from_yk(3, h)

    def third_line(h):
        @pl.when(end)
        def _():
            z1m(3, h).wait_recv()

        ykm(3, h).start()
        sib(6, h).start()
        from_yk(5, h)

    def new_0():
        own_new().wait()
        for k in range(1, heads):
            spread_in(k).wait_recv()
        ny().start()

    def new_1():
        ny().wait_recv()
        nz1(1).start()

        @pl.when(mid)
        def _():
            nz3(3).start()

        nsib(0).start()

    def new_2():
        nz1(1).wait_recv()
        nsib(1).start()

        @pl.when(mid)
        def _():
            nz3(2).start()
            nz3(3).wait_recv()
            nz1(2).start()

    def new_3():
        nz1(2).wait_recv()
        nsib(2).start()

        @pl.when(mid)
        def _():
            nz1(3).start()

    def new_4():
        @pl.when(end)
        def _():
            nz1(3).wait_recv()

        nsib(3).start()

    def prepare(chunk):
        if chunk == 0:
            waits = [sib(0, 0), sib(0, 1)]
        elif chunk == 7:
            waits = [sib(7, 0), sib(7, 1)]
        elif chunk < 7:
            k, h = (chunk + 1) // 2, (chunk + 1) % 2
            waits = [sib(2 * k - 1, h), sib(2 * k, h)]
        else:
            waits = [nsib(2 * (chunk - 8)), nsib(2 * (chunk - 8) + 1)]
        for w in waits:
            w.wait_recv()
        vt[chunk] = kv[chunk, :, HD:].T

    def partner_queries():
        qm(0).wait_recv()
        qm(1).wait_recv()
        place_queries(q_in, 1)

    def hand_back(t):
        cols = pl.ds((4 + t) * TILE, TILE)
        weight = jnp.sum(total[:, cols], 0, keepdims=True)
        so[t] = (acc[:, cols] / weight).astype(BF16)
        slse[t] = jnp.broadcast_to(top[:1, cols] + jnp.log2(weight), (8, TILE))
        om(t).start()
        lm(t).start()

    early = {
        1: [lambda: first_line(0), new_0],
        3: [new_1],
        5: [lambda: first_line(1)],
        6: [new_2],
        10: [lambda: second_line(0)],
        12: [new_3],
        13: [lambda: second_line(1)],
        17: [new_4],
        18: [lambda: third_line(0)],
        23: [lambda: third_line(1)],
        26: [lambda: from_yk(7, 0)],
        29: [lambda: from_yk(7, 1)],
        2 * LAST_PARTNER + 1: [lambda: hand_back(0), lambda: hand_back(1)],
        2 * LAST_PARTNER + 2: [lambda: hand_back(2), lambda: hand_back(3)],
    }
    late = {}
    seen, seen_owner = {0}, {0}
    for u, (chunk, owner) in enumerate(UNITS):
        todo = []
        if chunk not in seen:
            todo.append(functools.partial(prepare, chunk))
            seen.add(chunk)
        if owner not in seen_owner:
            todo.append(partner_queries)
            seen_owner.add(owner)
        if todo:
            late[2 * u - 1] = todo

    def perform(i, table):
        for k in sorted(table):
            @pl.when(i == k)
            def _():
                for action in table[k]:
                    action()

    def bias_of(chunk, tile, b):
        return bias[(jnp.maximum(chunk - 7, 0) * 2 + tile // 4) * 8 + b]

    def piece_scores(chunk, tile, buf, j):
        k = kv[chunk, pl.ds(j * PIECE, PIECE), :HD]
        cols = pl.ds(pl.multiple_of(tile * TILE, TILE), TILE)
        s = dot(jnp.concatenate([k, k], 1), qt[:, cols])
        best = None
        for b in range(PIECE // QD):
            part = s[b * QD : (b + 1) * QD]
            if j == 0 and b == 0:
                diagonal = jnp.where(jnp.logical_and(chunk == 8, tile < 4), 1, 0)
                part = part + tri[diagonal]
            scores[buf, pl.ds(j * PIECE + b * QD, QD), :] = part
            here = fold(part, jnp.maximum) - bias_of(chunk, tile, j * (PIECE // QD) + b)
            best = here if best is None else jnp.maximum(best, here)
        return best

    def step(chunk, tile, buf, chunk2, tile2):
        cols = pl.ds(pl.multiple_of(tile * TILE, TILE), TILE)
        old = top[:, cols]
        new = jnp.maximum(old, jnp.max(scores[buf, CHUNK:, :], 0, keepdims=True))
        shrink = jnp.exp2(old - new)
        top[:, cols] = new
        best = weight = value = None
        for j in range(CHUNK // PIECE):
            here = piece_scores(chunk2, tile2, 1 - buf, j)
            best = here if best is None else jnp.maximum(best, here)
            probs = []
            for b in range(PIECE // QD):
                shift = new + bias_of(chunk, tile, j * (PIECE // QD) + b)
                s = scores[buf, pl.ds(j * PIECE + b * QD, QD), :]
                p = jnp.exp2(s.reshape(QD // 8, 8, TILE) - shift[None]).reshape(QD, TILE)
                part = fold(p, jnp.add)
                weight = part if weight is None else weight + part
                probs.append(p.astype(BF16))
            part = dot(vt[chunk, :, pl.ds(j * PIECE, PIECE)], jnp.concatenate(probs, 0))
            value = part if value is None else value + part
        scores[1 - buf, CHUNK:, :] = best
        total[:, cols] = total[:, cols] * shrink + weight
        acc[:, cols] = acc[:, cols] * shrink[:1] + value

    chunks = [c for c, _ in UNITS] + [UNITS[-1][0]]
    owners = [o for _, o in UNITS] + [UNITS[-1][1]]

    prepare(0)
    first = None
    for j in range(CHUNK // PIECE):
        here = piece_scores(jnp.int32(0), jnp.int32(0), 0, j)
        first = here if first is None else jnp.maximum(first, here)
    scores[0, CHUNK:, :] = first

    def body(i, carry):
        u, second = i // 2, i % 2
        chunk, owner = lookup(u, chunks), lookup(u, owners)
        chunk2, owner2 = lookup(u + 1, chunks), lookup(u + 1, owners)
        tile = owner * 4 + second * 2
        perform(i, early)
        step(chunk, tile, 0, chunk, tile + 1)
        perform(i, late)
        chunk_n = jnp.where(second == 1, chunk2, chunk)
        tile_n = jnp.where(second == 1, owner2 * 4, tile + 2)
        step(chunk, tile + 1, 1, chunk_n, tile_n)
        return carry

    lax.fori_loop(0, 2 * len(UNITS), body, 0)

    for t in range(4):
        om(t).wait_recv()
        lm(t).wait_recv()
        cols = pl.ds(t * TILE, TILE)
        weight = jnp.sum(total[:, cols], 0, keepdims=True)
        mine = top[:1, cols] + jnp.log2(weight)
        theirs = plse[t][:1]
        best = jnp.maximum(mine, theirs)
        a, b = jnp.exp2(mine - best), jnp.exp2(theirs - best)
        norm = 1.0 / (a + b)
        result = acc[:, cols] * (a * norm / weight) + po[t].astype(F32) * (b * norm)
        for h in range(2):
            out_ref[:, pl.ds((2 * t + h) * HD, HD)] = result[:, h * HD : (h + 1) * HD].T.astype(BF16)

    for h in range(2):
        qm(h).wait_send()
        for slot in range(8):
            sib(slot, h).wait_send()
        for d in range(4):
            ykm(d, h).wait_send()
        z1m(1, h).wait_send()

        @pl.when(mid)
        def _():
            z1m(2, h).wait_send()
            z1m(3, h).wait_send()
            z3m(2, h).wait_send()
            z3m(3, h).wait_send()

    for k in range(1, heads):
        spread(k).wait_send()
    ny().wait_send()
    nz1(1).wait_send()
    for d in range(4):
        nsib(d).wait_send()
        om(d).wait_send()
        lm(d).wait_send()

    @pl.when(mid)
    def _():
        nz1(2).wait_send()
        nz1(3).wait_send()
        nz3(2).wait_send()
        nz3(3).wait_send()


def per_device(queries, cache, stretch_kv, stretch_pos):
    dma = pltpu.SemaphoreType.DMA
    vmem = pl.BlockSpec(memory_space=pltpu.VMEM)
    return pl.pallas_call(
        kernel,
        out_shape=jax.ShapeDtypeStruct(queries.shape, BF16),
        in_specs=[vmem, vmem, vmem, pl.BlockSpec(memory_space=pltpu.SMEM)],
        out_specs=vmem,
        scratch_shapes=[
            pltpu.VMEM((10, CHUNK, 2 * HD), BF16),
            pltpu.VMEM((10, HD, CHUNK), BF16),
            pltpu.VMEM((2 * HD, 2048), BF16),
            pltpu.VMEM((QD, 1024), BF16),
            pltpu.VMEM((2, CHUNK + 8, TILE), F32),
            pltpu.VMEM((HD, 2048), F32),
            pltpu.VMEM((8, 2048), F32),
            pltpu.VMEM((8, 2048), F32),
            pltpu.VMEM((2, QD, TILE), F32),
            pltpu.SMEM((48,), F32),
            pltpu.VMEM((4, HD, TILE), BF16),
            pltpu.VMEM((4, 8, TILE), F32),
            pltpu.VMEM((4, HD, TILE), BF16),
            pltpu.VMEM((4, 8, TILE), F32),
            dma((8, 2)), dma((8, 2)), dma((4, 2)), dma((8, 2)), dma((4, 2)), dma((4, 2)),
            dma((8,)), dma((8,)), dma((1,)), dma((1,)), dma((1,)), dma((4,)), dma((4,)), dma((4,)), dma((4,)), dma((4,)),
            dma((2,)), dma((2,)), dma((4, 2)), dma((4, 2)),
        ],
        compiler_params=pltpu.CompilerParams(
            collective_id=0, has_side_effects=True, vmem_limit_bytes=40 * 2**20
        ),
        cost_estimate=pl.CostEstimate(flops=11 * 10**9, bytes_accessed=2**20, transcendentals=21 * 10**6),
        name="attend",
    )(queries, cache, stretch_kv, stretch_pos)


def solution(mesh):
    return jax.shard_map(
        per_device,
        mesh=mesh,
        in_specs=(P("seq", "head"), P("seq", "head"), P(("seq", "head"), None), P()),
        out_specs=P("seq", "head"),
        check_vma=False,
    )
```

```python
import functools

import jax
import jax.numpy as jnp
from jax import lax
from jax.experimental import pallas as pl
from jax.experimental.pallas import tpu as pltpu
from jax.sharding import PartitionSpec as P

MESH = pl.DeviceIdType.MESH
F32, BF16 = jnp.float32, jnp.bfloat16
HD = 128
QD = 128
BLOCK = 512
TILE = 256
BIG = 1e30
A, B, X, Y = range(4)
KINDS = ((A, B), (X, Y), (B, X), (A, Y))
ROWS = (0, 0, 1, 2)
UNITS = (0, 4, 2, 3, 1, 6, 8, 7, 5, 10, 11, 9, 16, 18, 19, 12, 17, 14, 15, 13)
LATE = (1, 1, 1, 0, 0, 1, 1, 1, 0, 0, 1, 0, 0, 0, 1, 0, 0, 0, 1, 0)
ARRIVALS = (
    ("r0",),
    ("X0_0", "r1", "A1_0", "M_0", "A1_1", "M_1", "X0_1", "n0"),
    ("A2_0",),
    ("X1_0",),
    ("A2_1",),
    ("X1_1", "nX0"),
    ("n1", "X2_0"),
    ("n2",),
    ("X2_1",),
    ("n3", "nX1"),
    ("A3_0", "nX2"),
    (),
    ("nX3", "A3_1"),
    (),
    ("X3_0",),
    (),
    ("X3_1",),
    (),
    (),
    (),
    (),
)


def fold(x, op):
    parts = [x[8 * i : 8 * i + 8] for i in range(x.shape[0] // 8)]
    while len(parts) > 1:
        parts = [op(a, b) for a, b in zip(parts[::2], parts[1::2])]
    return parts[0]


def dot(a, b):
    return lax.dot_general(a, b, (((1,), (0,)), ((), ())), preferred_element_type=F32)


def choose(index, values):
    found = jnp.int32(values[0])
    for k, value in enumerate(values[1:], 1):
        found = jnp.where(index == k, jnp.int32(value), found)
    return found


def kernel(
    q_ref, cache_ref, new_ref, pos_ref, out_ref,
    kv, vt, qt, q_own, q_in, scores, acc, top, total, tri, bias, po, plse, so, slse,
    loc, siba_s, siba_r, sibx_s, sibx_r, y_s, y_r, z1_s, z3_s, z_r, all_s, all_r,
    nz_s, nz_r, nsa_s, nsa_r, nsx_s, nsx_r, ny_s, ny_r, q_s, q_r, o_s, o_r, l_s, l_r, met,
):
    me = lax.axis_index("seq")
    head = lax.axis_index("head")
    heads = 8
    core = me % 2
    y = (me // 2) % 4
    z = me // 8

    def seq(zz, yy, cc):
        return (zz * 4 + yy) * 2 + cc

    def at(zz, yy, cc):
        return {"seq": seq(zz, yy, cc)}

    ys = (y + 3 + 2 * core) % 4
    yr = (y + 5 - 2 * core) % 4
    z1 = z + 1 - 2 * (z % 2)
    z2 = (z + 2) % 4
    z3 = 3 - z
    other = 1 - core
    mid = jnp.logical_or(z == 1, z == 2)
    end = jnp.logical_or(z == 0, z == 3)
    to_sib, to_ys, to_yr = at(z, y, other), at(z, ys, core), at(z, yr, core)
    to_z1, to_z3 = at(z1, y, core), at(z3, y, core)

    def remote(src, dst, ss, rs, dev):
        return pltpu.make_async_remote_copy(
            src_ref=src, dst_ref=dst, send_sem=ss, recv_sem=rs, device_id=dev, device_id_type=MESH
        )

    def half(d, kind, h):
        return kv.at[4 * d + kind, pl.ds(h * 256, 256)]

    def own(h):
        return cache_ref.at[pl.ds(h * 256, 256)]

    def sib_a(d, h):
        src = half(d, A, h) if d else own(h)
        return remote(src, half(d, B, h), siba_s.at[d, h], siba_r.at[d, h], to_sib)

    def sib_x(d, h):
        return remote(half(d, X, h), half(d, Y, h), sibx_s.at[d, h], sibx_r.at[d, h], to_sib)

    def along_y(d, h):
        src = half(d, A, h) if d else own(h)
        return remote(src, half(d, X, h), y_s.at[d, h], y_r.at[d, h], to_ys)

    def outward(d, h):
        src = own(h) if d == 1 else half(5 - d, A, h)
        return remote(src, half(d, A, h), z1_s.at[d, h], z_r.at[d, h], to_z1)

    def inward(d, h):
        src = own(h) if d == 3 else half(1, A, h)
        return remote(src, half(d, A, h), z3_s.at[d, h], z_r.at[d, h], to_z3)

    def fresh(kind, d):
        return kv.at[16 + kind, pl.ds(d * QD, QD)]

    def spread(k):
        g = (head + k) % heads
        return remote(
            new_ref.at[:, pl.ds(pl.multiple_of(g * 256, 256), 256)],
            kv.at[16, pl.ds(pl.multiple_of(head * 16, 16), 16)],
            all_s.at[k], all_r.at[k], {"head": g},
        )

    def spread_in(k):
        g = (head + heads - k) % heads
        spot = kv.at[16, pl.ds(pl.multiple_of(g * 16, 16), 16)]
        return remote(spot, spot, all_s.at[k], all_r.at[k], {"head": g})

    def own_new():
        return pltpu.make_async_copy(
            new_ref.at[:, pl.ds(pl.multiple_of(head * 256, 256), 256)],
            kv.at[16, pl.ds(pl.multiple_of(head * 16, 16), 16)],
            loc.at[0],
        )

    def own_cache():
        return pltpu.make_async_copy(cache_ref, kv.at[0], loc.at[1])

    def own_queries():
        return pltpu.make_async_copy(q_ref, q_own, loc.at[2])

    def new_z(d):
        return remote(fresh(A, 0), fresh(A, d), nz_s.at[d], nz_r.at[d], {1: to_z1, 2: at(z2, y, core), 3: to_z3}[d])

    def new_y(d):
        return remote(fresh(A, d), fresh(X, d), ny_s.at[d], ny_r.at[d], to_ys)

    def new_sib_a(d):
        return remote(fresh(A, d), fresh(B, d), nsa_s.at[d], nsa_r.at[d], to_sib)

    def new_sib_x(d):
        return remote(fresh(X, d), fresh(Y, d), nsx_s.at[d], nsx_r.at[d], to_sib)

    def queries(s, h):
        cols = pl.ds(h * 512, 512)
        return remote(q_ref.at[:, cols], q_in.at[s, :, cols], q_s.at[s, h], q_r.at[s, h], to_ys if s else to_yr)

    def partial(s, t):
        return remote(so.at[s, t], po.at[1 - s, t], o_s.at[s, t], o_r.at[1 - s, t], to_yr if s else to_ys)

    def partial_log(s, t):
        return remote(slse.at[s, t], plse.at[1 - s, t], l_s.at[s, t], l_r.at[1 - s, t], to_yr if s else to_ys)

    own_cache().start()
    own_queries().start()
    own_new().start()
    barrier = pltpu.get_barrier_semaphore()
    x = head % 4
    height = (head // 4) * 4 + z

    def ring(k):
        up = (height + 8 + k) % 8
        return {"seq": seq(up % 4, y, core), "head": (up // 4) * 4 + x}

    row = [{"head": (head // 4) * 4 + (x + k) % 4} for k in range(1, 4)]
    peers = [to_sib, to_ys, to_yr, ring(1), ring(-1), ring(2), ring(-2)] + row
    for peer in peers:
        pl.semaphore_signal(barrier, inc=1, device_id=peer, device_id_type=MESH)

    key_at = lax.broadcasted_iota(jnp.int32, (QD, TILE), 0)
    row_at = lax.broadcasted_iota(jnp.int32, (QD, TILE), 1) % QD
    tri[0] = jnp.zeros((QD, TILE), F32)
    tri[1] = jnp.where(key_at <= row_at, 0.0, -BIG)
    row_pos = [pos_ref[me], pos_ref[seq(z, ys, core)], pos_ref[seq(z, yr, core)]]
    places = {A: (y, core), B: (y, other), X: (yr, core), Y: (ys, other)}
    for b in range(8):
        bias[b] = jnp.float32(0.0)
    for kind, blocks in enumerate(KINDS):
        for b in range(8):
            yy, cc = places[blocks[b // 4]]
            key_pos = pos_ref[seq((z, z1, z2, z3)[b % 4], yy, cc)]
            hidden = jnp.where(key_pos < row_pos[ROWS[kind]], 0.0, BIG).astype(F32)
            bias[(1 + kind) * 8 + b] = jnp.float32(0.0) if kind == 0 and b == 0 else hidden
    acc[...] = jnp.zeros_like(acc)
    top[...] = jnp.full_like(top, -BIG)
    total[...] = jnp.zeros_like(total)

    pl.semaphore_wait(barrier, len(peers))
    for h in range(2):
        outward(1, h).start()
        pl.when(mid)(lambda: inward(3, h).start())
        along_y(0, h).start()
        sib_a(0, h).start()
        for s in range(2):
            queries(s, h).start()

    def greet(k):
        for d in (2, -2):
            pl.semaphore_signal(met.at[k], inc=1, device_id=ring(d), device_id_type=MESH)

    greet(0)

    def place_queries(ref, rows):
        for h in range(8):
            q = ref[:, h * HD : (h + 1) * HD].astype(F32) * (HD ** -0.5 * 1.4426950408889634)
            high = q.astype(BF16)
            low = (q - high.astype(F32)).astype(BF16)
            tile, cols = rows * 4 + h // 2, pl.ds(h % 2 * HD, HD)
            qt[tile, :HD, cols] = high.T
            qt[tile, HD:, cols] = low.T

    own_queries().wait()
    place_queries(q_own, 0)
    own_cache().wait()

    def on_a(d, h):
        outward(d, h).wait_recv() if d < 3 else pl.when(end)(lambda: outward(3, h).wait_recv())
        along_y(d, h).start()
        sib_a(d, h).start()
        if d < 3:
            pl.when(mid)(lambda: (inward(2, h) if d == 1 else outward(3, h)).start())

    def on_mid(h):
        @pl.when(mid)
        def _():
            inward(3, h).wait_recv()
            outward(2, h).start()

    def on_x(d, h):
        along_y(d, h).wait_recv()
        sib_x(d, h).start()

    def on_new(d):
        if d == 0:
            own_new().wait()
            for k in range(1, heads):
                spread_in(k).wait_recv()
            for k in range(1, 4):
                new_z(k).start()
        else:
            new_z(d).wait_recv()
        new_y(d).start()
        new_sib_a(d).start()

    def on_new_x(d):
        new_y(d).wait_recv()
        new_sib_x(d).start()

    def on_round(k):
        pl.semaphore_wait(met.at[k], 2)
        if k == 0:
            greet(1)
        else:
            for g in range(1, heads):
                spread(g).start()

    def arrival(name):
        if name[0] == "A":
            on_a(int(name[1]), int(name[3]))
        elif name[0] == "M":
            on_mid(int(name[2]))
        elif name[0] == "X":
            on_x(int(name[1]), int(name[3]))
        elif name[0] == "r":
            on_round(int(name[1]))
        elif name[1] == "X":
            on_new_x(int(name[2]))
        else:
            on_new(int(name[1]))

    def prepare(block):
        d, kind = block // 4, block % 4
        if d < 4:
            waits = [] if kind in (A, X) else [(sib_a if kind == B else sib_x)(d, h) for h in range(2)]
        else:
            waits = [] if kind in (A, X) else [(new_sib_a if kind == B else new_sib_x)(k) for k in range(4)]
        for w in waits:
            w.wait_recv()
        vt[block] = kv[block, :, HD:].T

    def neighbour_queries():
        for s in range(2):
            for h in range(2):
                queries(s, h).wait_recv()
            place_queries(q_in.at[s], 1 + s)

    def hand_back(s):
        for t in range(4):
            tile = 4 * (1 + s) + t
            weight = jnp.sum(total[tile], 0, keepdims=True)
            so[s, t] = (acc[tile] / weight).astype(BF16)
            slse[s, t] = jnp.broadcast_to(top[tile][:1] + jnp.log2(weight), (8, TILE))
            partial(s, t).start()
            partial_log(s, t).start()

    def parts(unit):
        d, kind = unit // 4, unit % 4
        first = 4 * d + choose(kind, [k[0] for k in KINDS])
        second = 4 * d + choose(kind, [k[1] for k in KINDS])
        shift = jnp.where(d == 4, 1 + kind, 0) * 8
        return (first, second), choose(kind, ROWS) * 4, shift, jnp.where(unit == 16, 1, 0)

    def piece_scores(unit, t, buf, j):
        blocks, tile, shift, diagonal = unit
        k = kv[blocks[j], :, :HD]
        s = dot(jnp.concatenate([k, k], 1), qt[tile + t])
        best = None
        for b in range(BLOCK // QD):
            part = s[b * QD : (b + 1) * QD]
            if j == 0 and b == 0:
                part = part + tri[diagonal]
            scores[buf, pl.ds(j * BLOCK + b * QD, QD), :] = part
            here = fold(part, jnp.maximum) - bias[shift + j * (BLOCK // QD) + b]
            best = here if best is None else jnp.maximum(best, here)
        return best

    def step(unit, t, buf, unit2, t2):
        blocks, tile, shift, _ = unit
        tile = tile + t
        old = top[tile]
        new = jnp.maximum(old, jnp.max(scores[buf, 2 * BLOCK :, :], 0, keepdims=True))
        shrink = jnp.exp2(old - new)
        top[tile] = new
        best = weight = value = None
        for j in range(2):
            here = piece_scores(unit2, t2, 1 - buf, j)
            best = here if best is None else jnp.maximum(best, here)
            probs = []
            for b in range(BLOCK // QD):
                edge = new[:1] + bias[shift + j * (BLOCK // QD) + b]
                p = jnp.exp2(scores[buf, pl.ds(j * BLOCK + b * QD, QD), :] - edge)
                part = fold(p, jnp.add)
                weight = part if weight is None else weight + part
                probs.append(p.astype(BF16))
            part = dot(vt[blocks[j]], jnp.concatenate(probs, 0))
            value = part if value is None else value + part
        scores[1 - buf, 2 * BLOCK :, :] = best
        total[tile] = total[tile] * shrink + weight
        acc[tile] = acc[tile] * shrink[:1] + value

    def first_scores(unit):
        unit = parts(jnp.int32(unit))
        scores[0, 2 * BLOCK :, :] = jnp.maximum(piece_scores(unit, 0, 0, 0), piece_scores(unit, 0, 0, 1))

    todo = [[functools.partial(arrival, name) for name in names] for names in ARRIVALS]
    ready, asked = set(), False
    for u, unit in enumerate(UNITS):
        d, kind = unit // 4, unit % 4
        when = u if LATE[u] else u - 1
        for block in (4 * d + KINDS[kind][0], 4 * d + KINDS[kind][1]):
            if block not in ready:
                ready.add(block)
                todo[when].append(functools.partial(prepare, block))
        if ROWS[kind] and not asked:
            asked = True
            todo[when].append(neighbour_queries)
        if LATE[u]:
            todo[u].append(functools.partial(first_scores, unit))
    for s in range(2):
        last = max(u for u, unit in enumerate(UNITS) if ROWS[unit % 4] == 1 + s)
        todo[last + 1].append(functools.partial(hand_back, s))

    def body(u, carry):
        code = choose(u, UNITS)
        ahead = choose(u, [code if late else unit for unit, late, code in zip(UNITS[1:], LATE[1:], UNITS)] + [UNITS[-1]])
        for k, actions in enumerate(todo[: len(UNITS)]):
            if actions:
                @pl.when(u == k)
                def _():
                    for action in actions:
                        action()

        unit, unit2 = parts(code), parts(ahead)
        for t in range(4):
            step(unit, t, t % 2, unit if t < 3 else unit2, (t + 1) % 4)
        return carry

    lax.fori_loop(0, len(UNITS), body, 0)
    for action in todo[len(UNITS)]:
        action()

    for t in range(4):
        for s in range(2):
            partial(s, t).wait_recv()
            partial_log(s, t).wait_recv()
        weight = jnp.sum(total[t], 0, keepdims=True)
        logs = [top[t][:1] + jnp.log2(weight), plse[0, t][:1], plse[1, t][:1]]
        best = jnp.maximum(logs[0], jnp.maximum(logs[1], logs[2]))
        shares = [jnp.exp2(x - best) for x in logs]
        norm = 1.0 / (shares[0] + shares[1] + shares[2])
        result = acc[t] * (shares[0] * norm / weight)
        for s in range(2):
            result = result + po[s, t].astype(F32) * (shares[1 + s] * norm)
        for h in range(2):
            out_ref[:, pl.ds((2 * t + h) * HD, HD)] = result[:, h * HD : (h + 1) * HD].T.astype(BF16)

    for k in range(1, heads):
        spread(k).wait_send()
    for h in range(2):
        for d in range(4):
            sib_a(d, h).wait_send()
            sib_x(d, h).wait_send()
            along_y(d, h).wait_send()
        outward(1, h).wait_send()
        for s in range(2):
            queries(s, h).wait_send()
    for d in range(4):
        new_sib_a(d).wait_send()
        new_sib_x(d).wait_send()
        new_y(d).wait_send()
    for d in range(1, 4):
        new_z(d).wait_send()
    for s in range(2):
        for t in range(4):
            partial(s, t).wait_send()
            partial_log(s, t).wait_send()

    @pl.when(mid)
    def _():
        for h in range(2):
            outward(2, h).wait_send()
            outward(3, h).wait_send()
            inward(2, h).wait_send()
            inward(3, h).wait_send()


def per_device(queries, cache, stretch_kv, stretch_pos):
    dma = pltpu.SemaphoreType.DMA
    hbm = pl.BlockSpec(memory_space=pltpu.HBM)
    return pl.pallas_call(
        kernel,
        out_shape=jax.ShapeDtypeStruct(queries.shape, BF16),
        in_specs=[hbm, hbm, hbm, pl.BlockSpec(memory_space=pltpu.SMEM)],
        out_specs=pl.BlockSpec(memory_space=pltpu.VMEM),
        scratch_shapes=[
            pltpu.VMEM((20, BLOCK, 2 * HD), BF16),
            pltpu.VMEM((20, HD, BLOCK), BF16),
            pltpu.VMEM((12, 2 * HD, TILE), BF16),
            pltpu.VMEM((QD, 1024), BF16),
            pltpu.VMEM((2, QD, 1024), BF16),
            pltpu.VMEM((2, 2 * BLOCK + 8, TILE), F32),
            pltpu.VMEM((12, HD, TILE), F32),
            pltpu.VMEM((12, 8, TILE), F32),
            pltpu.VMEM((12, 8, TILE), F32),
            pltpu.VMEM((2, QD, TILE), F32),
            pltpu.SMEM((40,), F32),
            pltpu.VMEM((2, 4, HD, TILE), BF16),
            pltpu.VMEM((2, 4, 8, TILE), F32),
            pltpu.VMEM((2, 4, HD, TILE), BF16),
            pltpu.VMEM((2, 4, 8, TILE), F32),
            dma((3,)), dma((4, 2)), dma((4, 2)), dma((4, 2)), dma((4, 2)), dma((4, 2)), dma((4, 2)),
            dma((4, 2)), dma((4, 2)), dma((4, 2)), dma((8,)), dma((8,)),
            dma((4,)), dma((4,)), dma((4,)), dma((4,)), dma((4,)), dma((4,)), dma((4,)), dma((4,)),
            dma((2, 2)), dma((2, 2)), dma((2, 4)), dma((2, 4)), dma((2, 4)), dma((2, 4)),
            pltpu.SemaphoreType.REGULAR((2,)),
        ],
        compiler_params=pltpu.CompilerParams(
            collective_id=0, has_side_effects=True, vmem_limit_bytes=60 * 2**20
        ),
        cost_estimate=pl.CostEstimate(flops=11 * 10**9, bytes_accessed=2**20, transcendentals=21 * 10**6),
        name="attend",
    )(queries, cache, stretch_kv, stretch_pos)


def solution(mesh):
    return jax.shard_map(
        per_device,
        mesh=mesh,
        in_specs=(P("seq", "head"), P("seq", "head"), P(("seq", "head"), None), P()),
        out_specs=P("seq", "head"),
        check_vma=False,
    )
```

```python
import functools

import jax
import jax.numpy as jnp
from jax import lax
from jax.experimental import pallas as pl
from jax.experimental.pallas import tpu as pltpu
from jax.sharding import PartitionSpec as P

MESH = pl.DeviceIdType.MESH
F32, BF16 = jnp.float32, jnp.bfloat16
HD = 128
QD = 128
BLOCK = 512
TILE = 256
BIG = 1e30
A, B, X, Y = range(4)
KINDS = ((A, B), (X, Y), (B, X), (A, Y))
ROWS = (0, 0, 1, 2)
UNITS = (0, 4, 2, 3, 1, 6, 8, 7, 5, 10, 11, 14, 15, 18, 19, 9, 12, 13, 16, 17)
LATE = (1, 1, 1, 0, 0, 0, 1, 1, 0, 0, 1, 1, 1, 1, 1, 0, 0, 0, 0, 0)
ARRIVALS = (
    ("r0",),
    ("r1", "X0_0", "A1_0", "M_0", "r2", "r3", "A1_1", "M_1", "X0_1"),
    ("A2_0",),
    ("X1_0",),
    ("A2_1", "X1_1"),
    (),
    ("n0", "X2_0"),
    ("A3_0",),
    ("X2_1",),
    ("nX0", "A3_1"),
    (),
    ("n1", "X3_0", "n2", "X3_1"),
    ("n3", "nX1"),
    ("nX2", "nX3"),
    (),
    (),
    (),
    (),
    (),
    (),
    (),
)


def fold(x, op):
    parts = [x[8 * i : 8 * i + 8] for i in range(x.shape[0] // 8)]
    while len(parts) > 1:
        parts = [op(a, b) for a, b in zip(parts[::2], parts[1::2])]
    return parts[0]


def dot(a, b):
    return lax.dot_general(a, b, (((1,), (0,)), ((), ())), preferred_element_type=F32)


def choose(index, values):
    found = jnp.int32(values[0])
    for k, value in enumerate(values[1:], 1):
        found = jnp.where(index == k, jnp.int32(value), found)
    return found


def kernel(
    q_ref, cache_ref, new_ref, pos_ref, out_ref,
    kv, vt, qt, q_own, q_in, scores, acc, top, total, tri, bias, po, plse, so, slse,
    loc, siba_s, siba_r, sibx_s, sibx_r, y_s, y_r, z1_s, z3_s, z_r, all_s, all_r,
    nz_s, nz_r, nsa_s, nsa_r, nsx_s, nsx_r, ny_s, ny_r, q_s, q_r, o_s, o_r, l_s, l_r, met,
):
    me = lax.axis_index("seq")
    head = lax.axis_index("head")
    heads = 8
    core = me % 2
    y = (me // 2) % 4
    z = me // 8

    def seq(zz, yy, cc):
        return (zz * 4 + yy) * 2 + cc

    def at(zz, yy, cc):
        return {"seq": seq(zz, yy, cc)}

    ys = (y + 3 + 2 * core) % 4
    yr = (y + 5 - 2 * core) % 4
    z1 = z + 1 - 2 * (z % 2)
    z2 = (z + 2) % 4
    z3 = 3 - z
    other = 1 - core
    mid = jnp.logical_or(z == 1, z == 2)
    end = jnp.logical_or(z == 0, z == 3)
    to_sib, to_ys, to_yr = at(z, y, other), at(z, ys, core), at(z, yr, core)
    to_z1, to_z3 = at(z1, y, core), at(z3, y, core)

    def remote(src, dst, ss, rs, dev):
        return pltpu.make_async_remote_copy(
            src_ref=src, dst_ref=dst, send_sem=ss, recv_sem=rs, device_id=dev, device_id_type=MESH
        )

    def half(d, kind, h):
        return kv.at[4 * d + kind, pl.ds(h * 256, 256)]

    def own(h):
        return cache_ref.at[pl.ds(h * 256, 256)]

    def sib_a(d, h):
        src = half(d, A, h) if d else own(h)
        return remote(src, half(d, B, h), siba_s.at[d, h], siba_r.at[d, h], to_sib)

    def sib_x(d, h):
        return remote(half(d, X, h), half(d, Y, h), sibx_s.at[d, h], sibx_r.at[d, h], to_sib)

    def along_y(d, h):
        src = half(d, A, h) if d else own(h)
        return remote(src, half(d, X, h), y_s.at[d, h], y_r.at[d, h], to_ys)

    def outward(d, h):
        src = own(h) if d == 1 else half(5 - d, A, h)
        return remote(src, half(d, A, h), z1_s.at[d, h], z_r.at[d, h], to_z1)

    def inward(d, h):
        src = own(h) if d == 3 else half(1, A, h)
        return remote(src, half(d, A, h), z3_s.at[d, h], z_r.at[d, h], to_z3)

    def fresh(kind, d):
        return kv.at[16 + kind, pl.ds(d * QD, QD)]

    def spread(k):
        g = (head + k) % heads
        return remote(
            new_ref.at[:, pl.ds(pl.multiple_of(g * 256, 256), 256)],
            kv.at[16, pl.ds(pl.multiple_of(head * 16, 16), 16)],
            all_s.at[k], all_r.at[k], {"head": g},
        )

    def spread_in(k):
        g = (head + heads - k) % heads
        spot = kv.at[16, pl.ds(pl.multiple_of(g * 16, 16), 16)]
        return remote(spot, spot, all_s.at[k], all_r.at[k], {"head": g})

    def own_new():
        return pltpu.make_async_copy(
            new_ref.at[:, pl.ds(pl.multiple_of(head * 256, 256), 256)],
            kv.at[16, pl.ds(pl.multiple_of(head * 16, 16), 16)],
            loc.at[0],
        )

    def own_cache():
        return pltpu.make_async_copy(cache_ref, kv.at[0], loc.at[1])

    def own_queries():
        return pltpu.make_async_copy(q_ref, q_own, loc.at[2])

    def new_z(d):
        return remote(fresh(A, 0), fresh(A, d), nz_s.at[d], nz_r.at[d], {1: to_z1, 2: at(z2, y, core), 3: to_z3}[d])

    def new_y(d):
        return remote(fresh(A, d), fresh(X, d), ny_s.at[d], ny_r.at[d], to_ys)

    def new_sib_a(d):
        return remote(fresh(A, d), fresh(B, d), nsa_s.at[d], nsa_r.at[d], to_sib)

    def new_sib_x(d):
        return remote(fresh(X, d), fresh(Y, d), nsx_s.at[d], nsx_r.at[d], to_sib)

    def queries(s, h):
        cols = pl.ds(h * 512, 512)
        return remote(q_ref.at[:, cols], q_in.at[s, :, cols], q_s.at[s, h], q_r.at[s, h], to_ys if s else to_yr)

    def partial(s, t):
        return remote(so.at[s, t], po.at[1 - s, t], o_s.at[s, t], o_r.at[1 - s, t], to_yr if s else to_ys)

    def partial_log(s, t):
        return remote(slse.at[s, t], plse.at[1 - s, t], l_s.at[s, t], l_r.at[1 - s, t], to_yr if s else to_ys)

    own_cache().start()
    own_queries().start()
    own_new().start()
    barrier = pltpu.get_barrier_semaphore()
    x = head % 4
    height = (head // 4) * 4 + z

    def line(k):
        up = (height + 8 + k) % 8
        return {"seq": seq(up % 4, y, core), "head": (up // 4) * 4 + x}

    def greet(sem):
        @pl.when(height < 7)
        def _():
            pl.semaphore_signal(sem, inc=1, device_id=line(1), device_id_type=MESH)

        @pl.when(height > 0)
        def _():
            pl.semaphore_signal(sem, inc=1, device_id=line(-1), device_id_type=MESH)

    adjoining = jnp.where(jnp.logical_or(height == 0, height == 7), 1, 2)
    peers = [to_sib, to_ys, to_yr] + [{"head": (head // 4) * 4 + (x + k) % 4} for k in range(1, 4)]
    for peer in peers:
        pl.semaphore_signal(barrier, inc=1, device_id=peer, device_id_type=MESH)
    greet(barrier)

    key_at = lax.broadcasted_iota(jnp.int32, (QD, TILE), 0)
    row_at = lax.broadcasted_iota(jnp.int32, (QD, TILE), 1) % QD
    tri[0] = jnp.zeros((QD, TILE), F32)
    tri[1] = jnp.where(key_at <= row_at, 0.0, -BIG)
    row_pos = [pos_ref[me], pos_ref[seq(z, ys, core)], pos_ref[seq(z, yr, core)]]
    places = {A: (y, core), B: (y, other), X: (yr, core), Y: (ys, other)}
    for b in range(8):
        bias[b] = jnp.float32(0.0)
    for kind, blocks in enumerate(KINDS):
        for b in range(8):
            yy, cc = places[blocks[b // 4]]
            key_pos = pos_ref[seq((z, z1, z2, z3)[b % 4], yy, cc)]
            hidden = jnp.where(key_pos < row_pos[ROWS[kind]], 0.0, BIG).astype(F32)
            bias[(1 + kind) * 8 + b] = jnp.float32(0.0) if kind == 0 and b == 0 else hidden
    acc[...] = jnp.zeros_like(acc)
    top[...] = jnp.full_like(top, -BIG)
    total[...] = jnp.zeros_like(total)

    pl.semaphore_wait(barrier, len(peers) + adjoining)
    for h in range(2):
        outward(1, h).start()
        pl.when(mid)(lambda: inward(3, h).start())
        along_y(0, h).start()
        sib_a(0, h).start()
        for s in range(2):
            queries(s, h).start()

    greet(met.at[0])

    def place_queries(ref, rows):
        for h in range(8):
            q = ref[:, h * HD : (h + 1) * HD].astype(F32) * (HD ** -0.5 * 1.4426950408889634)
            high = q.astype(BF16)
            low = (q - high.astype(F32)).astype(BF16)
            tile, cols = rows * 4 + h // 2, pl.ds(h % 2 * HD, HD)
            qt[tile, :HD, cols] = high.T
            qt[tile, HD:, cols] = low.T

    own_queries().wait()
    place_queries(q_own, 0)
    own_cache().wait()

    def on_a(d, h):
        outward(d, h).wait_recv() if d < 3 else pl.when(end)(lambda: outward(3, h).wait_recv())
        along_y(d, h).start()
        sib_a(d, h).start()
        if d < 3:
            pl.when(mid)(lambda: (inward(2, h) if d == 1 else outward(3, h)).start())

    def on_mid(h):
        @pl.when(mid)
        def _():
            inward(3, h).wait_recv()
            outward(2, h).start()

    def on_x(d, h):
        along_y(d, h).wait_recv()
        sib_x(d, h).start()

    def on_new(d):
        if d == 0:
            own_new().wait()
            for k in range(1, heads):
                spread_in(k).wait_recv()
            for k in range(1, 4):
                new_z(k).start()
        else:
            new_z(d).wait_recv()
        new_y(d).start()
        new_sib_a(d).start()

    def on_new_x(d):
        new_y(d).wait_recv()
        new_sib_x(d).start()

    def on_round(k):
        pl.semaphore_wait(met.at[k], adjoining)
        if k < 3:
            greet(met.at[k + 1])
        else:
            for g in range(1, heads):
                spread(g).start()

    def arrival(name):
        if name[0] == "A":
            on_a(int(name[1]), int(name[3]))
        elif name[0] == "M":
            on_mid(int(name[2]))
        elif name[0] == "X":
            on_x(int(name[1]), int(name[3]))
        elif name[0] == "r":
            on_round(int(name[1]))
        elif name[1] == "X":
            on_new_x(int(name[2]))
        else:
            on_new(int(name[1]))

    def prepare(block):
        d, kind = block // 4, block % 4
        if d < 4:
            waits = [] if kind in (A, X) else [(sib_a if kind == B else sib_x)(d, h) for h in range(2)]
        else:
            waits = [] if kind in (A, X) else [(new_sib_a if kind == B else new_sib_x)(k) for k in range(4)]
        for w in waits:
            w.wait_recv()
        vt[block] = kv[block, :, HD:].T

    def neighbour_queries():
        for s in range(2):
            for h in range(2):
                queries(s, h).wait_recv()
            place_queries(q_in.at[s], 1 + s)

    def hand_back(s):
        for t in range(4):
            tile = 4 * (1 + s) + t
            weight = jnp.sum(total[tile], 0, keepdims=True)
            so[s, t] = (acc[tile] / weight).astype(BF16)
            slse[s, t] = jnp.broadcast_to(top[tile][:1] + jnp.log2(weight), (8, TILE))
            partial(s, t).start()
            partial_log(s, t).start()

    def parts(unit):
        d, kind = unit // 4, unit % 4
        first = 4 * d + choose(kind, [k[0] for k in KINDS])
        second = 4 * d + choose(kind, [k[1] for k in KINDS])
        shift = jnp.where(d == 4, 1 + kind, 0) * 8
        return (first, second), choose(kind, ROWS) * 4, shift, jnp.where(unit == 16, 1, 0)

    def piece_scores(unit, t, buf, j):
        blocks, tile, shift, diagonal = unit
        k = kv[blocks[j], :, :HD]
        s = dot(jnp.concatenate([k, k], 1), qt[tile + t])
        best = None
        for b in range(BLOCK // QD):
            part = s[b * QD : (b + 1) * QD]
            if j == 0 and b == 0:
                part = part + tri[diagonal]
            scores[buf, pl.ds(j * BLOCK + b * QD, QD), :] = part
            here = fold(part, jnp.maximum) - bias[shift + j * (BLOCK // QD) + b]
            best = here if best is None else jnp.maximum(best, here)
        return best

    def step(unit, t, buf, unit2, t2):
        blocks, tile, shift, _ = unit
        tile = tile + t
        old = top[tile]
        new = jnp.maximum(old, jnp.max(scores[buf, 2 * BLOCK :, :], 0, keepdims=True))
        shrink = jnp.exp2(old - new)
        top[tile] = new
        best = weight = value = None
        for j in range(2):
            here = piece_scores(unit2, t2, 1 - buf, j)
            best = here if best is None else jnp.maximum(best, here)
            probs = []
            for b in range(BLOCK // QD):
                edge = new[:1] + bias[shift + j * (BLOCK // QD) + b]
                p = jnp.exp2(scores[buf, pl.ds(j * BLOCK + b * QD, QD), :] - edge)
                part = fold(p, jnp.add)
                weight = part if weight is None else weight + part
                probs.append(p.astype(BF16))
            part = dot(vt[blocks[j]], jnp.concatenate(probs, 0))
            value = part if value is None else value + part
        scores[1 - buf, 2 * BLOCK :, :] = best
        total[tile] = total[tile] * shrink + weight
        acc[tile] = acc[tile] * shrink[:1] + value

    def first_scores(unit):
        unit = parts(jnp.int32(unit))
        scores[0, 2 * BLOCK :, :] = jnp.maximum(piece_scores(unit, 0, 0, 0), piece_scores(unit, 0, 0, 1))

    todo = [[functools.partial(arrival, name) for name in names] for names in ARRIVALS]
    ready, asked = set(), False
    for u, unit in enumerate(UNITS):
        d, kind = unit // 4, unit % 4
        when = u if LATE[u] else u - 1
        for block in (4 * d + KINDS[kind][0], 4 * d + KINDS[kind][1]):
            if block not in ready:
                ready.add(block)
                todo[when].append(functools.partial(prepare, block))
        if ROWS[kind] and not asked:
            asked = True
            todo[when].append(neighbour_queries)
        if LATE[u]:
            todo[u].append(functools.partial(first_scores, unit))
    for s in range(2):
        last = max(u for u, unit in enumerate(UNITS) if ROWS[unit % 4] == 1 + s)
        todo[last + 1].append(functools.partial(hand_back, s))

    def body(u, carry):
        code = choose(u, UNITS)
        ahead = choose(u, [code if late else unit for unit, late, code in zip(UNITS[1:], LATE[1:], UNITS)] + [UNITS[-1]])
        for k, actions in enumerate(todo[: len(UNITS)]):
            if actions:
                @pl.when(u == k)
                def _():
                    for action in actions:
                        action()

        unit, unit2 = parts(code), parts(ahead)
        for t in range(4):
            step(unit, t, t % 2, unit if t < 3 else unit2, (t + 1) % 4)
        return carry

    lax.fori_loop(0, len(UNITS), body, 0)
    for action in todo[len(UNITS)]:
        action()

    for t in range(4):
        for s in range(2):
            partial(s, t).wait_recv()
            partial_log(s, t).wait_recv()
        weight = jnp.sum(total[t], 0, keepdims=True)
        logs = [top[t][:1] + jnp.log2(weight), plse[0, t][:1], plse[1, t][:1]]
        best = jnp.maximum(logs[0], jnp.maximum(logs[1], logs[2]))
        shares = [jnp.exp2(x - best) for x in logs]
        norm = 1.0 / (shares[0] + shares[1] + shares[2])
        result = acc[t] * (shares[0] * norm / weight)
        for s in range(2):
            result = result + po[s, t].astype(F32) * (shares[1 + s] * norm)
        for h in range(2):
            out_ref[:, pl.ds((2 * t + h) * HD, HD)] = result[:, h * HD : (h + 1) * HD].T.astype(BF16)

    for k in range(1, heads):
        spread(k).wait_send()
    for h in range(2):
        for d in range(4):
            sib_a(d, h).wait_send()
            sib_x(d, h).wait_send()
            along_y(d, h).wait_send()
        outward(1, h).wait_send()
        for s in range(2):
            queries(s, h).wait_send()
    for d in range(4):
        new_sib_a(d).wait_send()
        new_sib_x(d).wait_send()
        new_y(d).wait_send()
    for d in range(1, 4):
        new_z(d).wait_send()
    for s in range(2):
        for t in range(4):
            partial(s, t).wait_send()
            partial_log(s, t).wait_send()

    @pl.when(mid)
    def _():
        for h in range(2):
            outward(2, h).wait_send()
            outward(3, h).wait_send()
            inward(2, h).wait_send()
            inward(3, h).wait_send()


def per_device(queries, cache, stretch_kv, stretch_pos):
    dma = pltpu.SemaphoreType.DMA
    hbm = pl.BlockSpec(memory_space=pltpu.HBM)
    return pl.pallas_call(
        kernel,
        out_shape=pltpu.VMEM(queries.shape, BF16),
        in_specs=[hbm, hbm, hbm, pl.BlockSpec(memory_space=pltpu.SMEM)],
        out_specs=pl.BlockSpec(memory_space=pltpu.VMEM),
        scratch_shapes=[
            pltpu.VMEM((20, BLOCK, 2 * HD), BF16),
            pltpu.VMEM((20, HD, BLOCK), BF16),
            pltpu.VMEM((12, 2 * HD, TILE), BF16),
            pltpu.VMEM((QD, 1024), BF16),
            pltpu.VMEM((2, QD, 1024), BF16),
            pltpu.VMEM((2, 2 * BLOCK + 8, TILE), F32),
            pltpu.VMEM((12, HD, TILE), F32),
            pltpu.VMEM((12, 8, TILE), F32),
            pltpu.VMEM((12, 8, TILE), F32),
            pltpu.VMEM((2, QD, TILE), F32),
            pltpu.SMEM((40,), F32),
            pltpu.VMEM((2, 4, HD, TILE), BF16),
            pltpu.VMEM((2, 4, 8, TILE), F32),
            pltpu.VMEM((2, 4, HD, TILE), BF16),
            pltpu.VMEM((2, 4, 8, TILE), F32),
            dma((3,)), dma((4, 2)), dma((4, 2)), dma((4, 2)), dma((4, 2)), dma((4, 2)), dma((4, 2)),
            dma((4, 2)), dma((4, 2)), dma((4, 2)), dma((8,)), dma((8,)),
            dma((4,)), dma((4,)), dma((4,)), dma((4,)), dma((4,)), dma((4,)), dma((4,)), dma((4,)),
            dma((2, 2)), dma((2, 2)), dma((2, 4)), dma((2, 4)), dma((2, 4)), dma((2, 4)),
            pltpu.SemaphoreType.REGULAR((4,)),
        ],
        compiler_params=pltpu.CompilerParams(
            collective_id=0, has_side_effects=True, vmem_limit_bytes=60 * 2**20
        ),
        cost_estimate=pl.CostEstimate(flops=11 * 10**9, bytes_accessed=2**20, transcendentals=21 * 10**6),
        name="attend",
    )(queries, cache, stretch_kv, stretch_pos)


def solution(mesh):
    return jax.shard_map(
        per_device,
        mesh=mesh,
        in_specs=(P("seq", "head"), P("seq", "head"), P(("seq", "head"), None), P()),
        out_specs=P("seq", "head"),
        check_vma=False,
    )
```

```python
import functools

import jax
import jax.numpy as jnp
from jax import lax
from jax.experimental import pallas as pl
from jax.experimental.pallas import tpu as pltpu
from jax.sharding import PartitionSpec as P

MESH = pl.DeviceIdType.MESH
F32, BF16 = jnp.float32, jnp.bfloat16
HD = 128
QD = 128
BLOCK = 512
TILE = 256
BIG = 1e30
A, B, X, Y = range(4)
KINDS = ((A, B), (X, Y), (B, X), (A, Y))
ROWS = (0, 0, 1, 2)
UNITS = (0, 4, 2, 3, 1, 6, 8, 7, 5, 10, 11, 14, 15, 18, 19, 9, 12, 13, 16, 17)
LATE = (1, 1, 1, 0, 0, 0, 1, 1, 0, 0, 1, 1, 1, 1, 1, 0, 0, 0, 0, 0)
ARRIVALS = (
    ("r0",),
    ("r1", "X0_0", "A1_0", "M_0", "r2", "r3", "A1_1", "M_1", "X0_1"),
    ("A2_0",),
    ("X1_0",),
    ("A2_1", "X1_1"),
    (),
    ("n0", "X2_0"),
    ("A3_0",),
    ("X2_1",),
    ("nX0", "A3_1"),
    (),
    ("n1", "X3_0", "n2", "X3_1"),
    ("n3", "nX1"),
    ("nX2", "nX3"),
    (),
    (),
    (),
    (),
    (),
    (),
    (),
)


def fold(x, op):
    parts = [x[8 * i : 8 * i + 8] for i in range(x.shape[0] // 8)]
    while len(parts) > 1:
        parts = [op(a, b) for a, b in zip(parts[::2], parts[1::2])]
    return parts[0]


def dot(a, b):
    return lax.dot_general(a, b, (((1,), (0,)), ((), ())), preferred_element_type=F32)


def choose(index, values):
    found = jnp.int32(values[0])
    for k, value in enumerate(values[1:], 1):
        found = jnp.where(index == k, jnp.int32(value), found)
    return found


def kernel(
    q_ref, cache_ref, new_ref, pos_ref, out_ref,
    kv, vt, qt, q_own, q_in, scores, acc, top, total, tri, bias, po, plse, so, slse,
    loc, siba_s, siba_r, sibx_s, sibx_r, y_s, y_r, z1_s, z3_s, z_r, all_s, all_r,
    nz_s, nz_r, nsa_s, nsa_r, nsx_s, nsx_r, ny_s, ny_r, q_s, q_r, o_s, o_r, l_s, l_r, met,
):
    me = lax.axis_index("seq")
    head = lax.axis_index("head")
    heads = 8
    core = me % 2
    y = (me // 2) % 4
    z = me // 8

    def seq(zz, yy, cc):
        return (zz * 4 + yy) * 2 + cc

    def at(zz, yy, cc):
        return {"seq": seq(zz, yy, cc)}

    ys = (y + 3 + 2 * core) % 4
    yr = (y + 5 - 2 * core) % 4
    z1 = z + 1 - 2 * (z % 2)
    z2 = (z + 2) % 4
    z3 = 3 - z
    other = 1 - core
    mid = jnp.logical_or(z == 1, z == 2)
    end = jnp.logical_or(z == 0, z == 3)
    to_sib, to_ys, to_yr = at(z, y, other), at(z, ys, core), at(z, yr, core)
    to_z1, to_z3 = at(z1, y, core), at(z3, y, core)

    def remote(src, dst, ss, rs, dev):
        return pltpu.make_async_remote_copy(
            src_ref=src, dst_ref=dst, send_sem=ss, recv_sem=rs, device_id=dev, device_id_type=MESH
        )

    def half(d, kind, h):
        return kv.at[4 * d + kind, pl.ds(h * 256, 256)]

    def own(h):
        return cache_ref.at[pl.ds(h * 256, 256)]

    def sib_a(d, h):
        src = half(d, A, h) if d else own(h)
        return remote(src, half(d, B, h), siba_s.at[d, h], siba_r.at[d, h], to_sib)

    def sib_x(d, h):
        return remote(half(d, X, h), half(d, Y, h), sibx_s.at[d, h], sibx_r.at[d, h], to_sib)

    def along_y(d, h):
        src = half(d, A, h) if d else own(h)
        return remote(src, half(d, X, h), y_s.at[d, h], y_r.at[d, h], to_ys)

    def outward(d, h):
        src = own(h) if d == 1 else half(5 - d, A, h)
        return remote(src, half(d, A, h), z1_s.at[d, h], z_r.at[d, h], to_z1)

    def inward(d, h):
        src = own(h) if d == 3 else half(1, A, h)
        return remote(src, half(d, A, h), z3_s.at[d, h], z_r.at[d, h], to_z3)

    def fresh(kind, d):
        return kv.at[16 + kind, pl.ds(d * QD, QD)]

    def spread(k):
        g = (head + k) % heads
        return remote(
            new_ref.at[:, pl.ds(pl.multiple_of(g * 256, 256), 256)],
            kv.at[16, pl.ds(pl.multiple_of(head * 16, 16), 16)],
            all_s.at[k], all_r.at[k], {"head": g},
        )

    def spread_in(k):
        g = (head + heads - k) % heads
        spot = kv.at[16, pl.ds(pl.multiple_of(g * 16, 16), 16)]
        return remote(spot, spot, all_s.at[k], all_r.at[k], {"head": g})

    def own_new():
        return pltpu.make_async_copy(
            new_ref.at[:, pl.ds(pl.multiple_of(head * 256, 256), 256)],
            kv.at[16, pl.ds(pl.multiple_of(head * 16, 16), 16)],
            loc.at[0],
        )

    def own_cache():
        return pltpu.make_async_copy(cache_ref, kv.at[0], loc.at[1])

    def own_queries():
        return pltpu.make_async_copy(q_ref, q_own, loc.at[2])

    def new_z(d):
        return remote(fresh(A, 0), fresh(A, d), nz_s.at[d], nz_r.at[d], {1: to_z1, 2: at(z2, y, core), 3: to_z3}[d])

    def new_y(d):
        return remote(fresh(A, d), fresh(X, d), ny_s.at[d], ny_r.at[d], to_ys)

    def new_sib_a(d):
        return remote(fresh(A, d), fresh(B, d), nsa_s.at[d], nsa_r.at[d], to_sib)

    def new_y_other(d):
        return remote(fresh(A, d), fresh(Y, d), nsx_s.at[d], nsx_r.at[d], at(z, ys, other))

    def queries(s, h):
        cols = pl.ds(h * 512, 512)
        return remote(q_ref.at[:, cols], q_in.at[s, :, cols], q_s.at[s, h], q_r.at[s, h], to_ys if s else to_yr)

    def partial(s, t):
        return remote(so.at[s, t], po.at[1 - s, t], o_s.at[s, t], o_r.at[1 - s, t], to_yr if s else to_ys)

    def partial_log(s, t):
        return remote(slse.at[s, t], plse.at[1 - s, t], l_s.at[s, t], l_r.at[1 - s, t], to_yr if s else to_ys)

    own_cache().start()
    own_queries().start()
    own_new().start()
    barrier = pltpu.get_barrier_semaphore()
    x = head % 4
    height = (head // 4) * 4 + z

    def line(k):
        up = (height + 8 + k) % 8
        return {"seq": seq(up % 4, y, core), "head": (up // 4) * 4 + x}

    def greet(sem):
        @pl.when(height < 7)
        def _():
            pl.semaphore_signal(sem, inc=1, device_id=line(1), device_id_type=MESH)

        @pl.when(height > 0)
        def _():
            pl.semaphore_signal(sem, inc=1, device_id=line(-1), device_id_type=MESH)

    adjoining = jnp.where(jnp.logical_or(height == 0, height == 7), 1, 2)
    peers = [to_sib, to_ys, to_yr] + [{"head": (head // 4) * 4 + (x + k) % 4} for k in range(1, 4)]
    for peer in peers:
        pl.semaphore_signal(barrier, inc=1, device_id=peer, device_id_type=MESH)
    greet(barrier)

    key_at = lax.broadcasted_iota(jnp.int32, (QD, TILE), 0)
    row_at = lax.broadcasted_iota(jnp.int32, (QD, TILE), 1) % QD
    tri[0] = jnp.zeros((QD, TILE), F32)
    tri[1] = jnp.where(key_at <= row_at, 0.0, -BIG)
    row_pos = [pos_ref[me], pos_ref[seq(z, ys, core)], pos_ref[seq(z, yr, core)]]
    places = {A: (y, core), B: (y, other), X: (yr, core), Y: (ys, other)}
    for b in range(8):
        bias[b] = jnp.float32(0.0)
    for kind, blocks in enumerate(KINDS):
        for b in range(8):
            yy, cc = places[blocks[b // 4]]
            key_pos = pos_ref[seq((z, z1, z2, z3)[b % 4], yy, cc)]
            hidden = jnp.where(key_pos < row_pos[ROWS[kind]], 0.0, BIG).astype(F32)
            bias[(1 + kind) * 8 + b] = jnp.float32(0.0) if kind == 0 and b == 0 else hidden
    acc[...] = jnp.zeros_like(acc)
    top[...] = jnp.full_like(top, -BIG)
    total[...] = jnp.zeros_like(total)

    pl.semaphore_wait(barrier, len(peers) + adjoining)
    for h in range(2):
        outward(1, h).start()
        pl.when(mid)(lambda: inward(3, h).start())
        along_y(0, h).start()
        sib_a(0, h).start()
        for s in range(2):
            queries(s, h).start()

    greet(met.at[0])

    def place_queries(ref, rows):
        for h in range(8):
            q = ref[:, h * HD : (h + 1) * HD].astype(F32) * (HD ** -0.5 * 1.4426950408889634)
            high = q.astype(BF16)
            low = (q - high.astype(F32)).astype(BF16)
            tile, cols = rows * 4 + h // 2, pl.ds(h % 2 * HD, HD)
            qt[tile, :HD, cols] = high.T
            qt[tile, HD:, cols] = low.T

    own_queries().wait()
    place_queries(q_own, 0)
    own_cache().wait()

    def on_a(d, h):
        outward(d, h).wait_recv() if d < 3 else pl.when(end)(lambda: outward(3, h).wait_recv())
        along_y(d, h).start()
        sib_a(d, h).start()
        if d < 3:
            pl.when(mid)(lambda: (inward(2, h) if d == 1 else outward(3, h)).start())

    def on_mid(h):
        @pl.when(mid)
        def _():
            inward(3, h).wait_recv()
            outward(2, h).start()

    def on_x(d, h):
        along_y(d, h).wait_recv()
        sib_x(d, h).start()

    def on_new(d):
        if d == 0:
            own_new().wait()
            for k in range(1, heads):
                spread_in(k).wait_recv()
            for k in range(1, 4):
                new_z(k).start()
        else:
            new_z(d).wait_recv()
        new_y(d).start()
        new_y_other(d).start()
        new_sib_a(d).start()

    def on_new_x(d):
        new_y(d).wait_recv()

    def on_round(k):
        pl.semaphore_wait(met.at[k], adjoining)
        if k < 3:
            greet(met.at[k + 1])
        else:
            for g in range(1, heads):
                spread(g).start()

    def arrival(name):
        if name[0] == "A":
            on_a(int(name[1]), int(name[3]))
        elif name[0] == "M":
            on_mid(int(name[2]))
        elif name[0] == "X":
            on_x(int(name[1]), int(name[3]))
        elif name[0] == "r":
            on_round(int(name[1]))
        elif name[1] == "X":
            on_new_x(int(name[2]))
        else:
            on_new(int(name[1]))

    def prepare(block):
        d, kind = block // 4, block % 4
        if d < 4:
            waits = [] if kind in (A, X) else [(sib_a if kind == B else sib_x)(d, h) for h in range(2)]
        else:
            waits = [] if kind in (A, X) else [(new_sib_a if kind == B else new_y_other)(k) for k in range(4)]
        for w in waits:
            w.wait_recv()
        vt[block] = kv[block, :, HD:].T

    def neighbour_queries():
        for s in range(2):
            for h in range(2):
                queries(s, h).wait_recv()
            place_queries(q_in.at[s], 1 + s)

    def hand_back(s):
        for t in range(4):
            tile = 4 * (1 + s) + t
            weight = jnp.sum(total[tile], 0, keepdims=True)
            so[s, t] = (acc[tile] / weight).astype(BF16)
            slse[s, t] = jnp.broadcast_to(top[tile][:1] + jnp.log2(weight), (8, TILE))
            partial(s, t).start()
            partial_log(s, t).start()

    def parts(unit):
        d, kind = unit // 4, unit % 4
        first = 4 * d + choose(kind, [k[0] for k in KINDS])
        second = 4 * d + choose(kind, [k[1] for k in KINDS])
        shift = jnp.where(d == 4, 1 + kind, 0) * 8
        return (first, second), choose(kind, ROWS) * 4, shift, jnp.where(unit == 16, 1, 0)

    def piece_scores(unit, t, buf, j):
        blocks, tile, shift, diagonal = unit
        k = kv[blocks[j], :, :HD]
        s = dot(jnp.concatenate([k, k], 1), qt[tile + t])
        best = None
        for b in range(BLOCK // QD):
            part = s[b * QD : (b + 1) * QD]
            if j == 0 and b == 0:
                part = part + tri[diagonal]
            scores[buf, pl.ds(j * BLOCK + b * QD, QD), :] = part
            here = fold(part, jnp.maximum) - bias[shift + j * (BLOCK // QD) + b]
            best = here if best is None else jnp.maximum(best, here)
        return best

    def step(unit, t, buf, unit2, t2):
        blocks, tile, shift, _ = unit
        tile = tile + t
        old = top[tile]
        new = jnp.maximum(old, jnp.max(scores[buf, 2 * BLOCK :, :], 0, keepdims=True))
        shrink = jnp.exp2(old - new)
        top[tile] = new
        best = weight = value = None
        for j in range(2):
            here = piece_scores(unit2, t2, 1 - buf, j)
            best = here if best is None else jnp.maximum(best, here)
            probs = []
            for b in range(BLOCK // QD):
                edge = new[:1] + bias[shift + j * (BLOCK // QD) + b]
                p = jnp.exp2(scores[buf, pl.ds(j * BLOCK + b * QD, QD), :] - edge)
                part = fold(p, jnp.add)
                weight = part if weight is None else weight + part
                probs.append(p.astype(BF16))
            part = dot(vt[blocks[j]], jnp.concatenate(probs, 0))
            value = part if value is None else value + part
        scores[1 - buf, 2 * BLOCK :, :] = best
        total[tile] = total[tile] * shrink + weight
        acc[tile] = acc[tile] * shrink[:1] + value

    def first_scores(unit):
        unit = parts(jnp.int32(unit))
        scores[0, 2 * BLOCK :, :] = jnp.maximum(piece_scores(unit, 0, 0, 0), piece_scores(unit, 0, 0, 1))

    todo = [[functools.partial(arrival, name) for name in names] for names in ARRIVALS]
    ready, asked = set(), False
    for u, unit in enumerate(UNITS):
        d, kind = unit // 4, unit % 4
        when = u if LATE[u] else u - 1
        for block in (4 * d + KINDS[kind][0], 4 * d + KINDS[kind][1]):
            if block not in ready:
                ready.add(block)
                todo[when].append(functools.partial(prepare, block))
        if ROWS[kind] and not asked:
            asked = True
            todo[when].append(neighbour_queries)
        if LATE[u]:
            todo[u].append(functools.partial(first_scores, unit))
    for s in range(2):
        last = max(u for u, unit in enumerate(UNITS) if ROWS[unit % 4] == 1 + s)
        todo[last + 1].append(functools.partial(hand_back, s))

    def body(u, carry):
        code = choose(u, UNITS)
        ahead = choose(u, [code if late else unit for unit, late, code in zip(UNITS[1:], LATE[1:], UNITS)] + [UNITS[-1]])
        for k, actions in enumerate(todo[: len(UNITS)]):
            if actions:
                @pl.when(u == k)
                def _():
                    for action in actions:
                        action()

        unit, unit2 = parts(code), parts(ahead)
        for t in range(4):
            step(unit, t, t % 2, unit if t < 3 else unit2, (t + 1) % 4)
        return carry

    lax.fori_loop(0, len(UNITS), body, 0)
    for action in todo[len(UNITS)]:
        action()

    for t in range(4):
        for s in range(2):
            partial(s, t).wait_recv()
            partial_log(s, t).wait_recv()
        weight = jnp.sum(total[t], 0, keepdims=True)
        logs = [top[t][:1] + jnp.log2(weight), plse[0, t][:1], plse[1, t][:1]]
        best = jnp.maximum(logs[0], jnp.maximum(logs[1], logs[2]))
        shares = [jnp.exp2(x - best) for x in logs]
        norm = 1.0 / (shares[0] + shares[1] + shares[2])
        result = acc[t] * (shares[0] * norm / weight)
        for s in range(2):
            result = result + po[s, t].astype(F32) * (shares[1 + s] * norm)
        for h in range(2):
            out_ref[:, pl.ds((2 * t + h) * HD, HD)] = result[:, h * HD : (h + 1) * HD].T.astype(BF16)

    for k in range(1, heads):
        spread(k).wait_send()
    for h in range(2):
        for d in range(4):
            sib_a(d, h).wait_send()
            sib_x(d, h).wait_send()
            along_y(d, h).wait_send()
        outward(1, h).wait_send()
        for s in range(2):
            queries(s, h).wait_send()
    for d in range(4):
        new_sib_a(d).wait_send()
        new_y_other(d).wait_send()
        new_y(d).wait_send()
    for d in range(1, 4):
        new_z(d).wait_send()
    for s in range(2):
        for t in range(4):
            partial(s, t).wait_send()
            partial_log(s, t).wait_send()

    @pl.when(mid)
    def _():
        for h in range(2):
            outward(2, h).wait_send()
            outward(3, h).wait_send()
            inward(2, h).wait_send()
            inward(3, h).wait_send()


def per_device(queries, cache, stretch_kv, stretch_pos):
    dma = pltpu.SemaphoreType.DMA
    hbm = pl.BlockSpec(memory_space=pltpu.HBM)
    return pl.pallas_call(
        kernel,
        out_shape=pltpu.VMEM(queries.shape, BF16),
        in_specs=[hbm, hbm, hbm, pl.BlockSpec(memory_space=pltpu.SMEM)],
        out_specs=pl.BlockSpec(memory_space=pltpu.VMEM),
        scratch_shapes=[
            pltpu.VMEM((20, BLOCK, 2 * HD), BF16),
            pltpu.VMEM((20, HD, BLOCK), BF16),
            pltpu.VMEM((12, 2 * HD, TILE), BF16),
            pltpu.VMEM((QD, 1024), BF16),
            pltpu.VMEM((2, QD, 1024), BF16),
            pltpu.VMEM((2, 2 * BLOCK + 8, TILE), F32),
            pltpu.VMEM((12, HD, TILE), F32),
            pltpu.VMEM((12, 8, TILE), F32),
            pltpu.VMEM((12, 8, TILE), F32),
            pltpu.VMEM((2, QD, TILE), F32),
            pltpu.SMEM((40,), F32),
            pltpu.VMEM((2, 4, HD, TILE), BF16),
            pltpu.VMEM((2, 4, 8, TILE), F32),
            pltpu.VMEM((2, 4, HD, TILE), BF16),
            pltpu.VMEM((2, 4, 8, TILE), F32),
            dma((3,)), dma((4, 2)), dma((4, 2)), dma((4, 2)), dma((4, 2)), dma((4, 2)), dma((4, 2)),
            dma((4, 2)), dma((4, 2)), dma((4, 2)), dma((8,)), dma((8,)),
            dma((4,)), dma((4,)), dma((4,)), dma((4,)), dma((4,)), dma((4,)), dma((4,)), dma((4,)),
            dma((2, 2)), dma((2, 2)), dma((2, 4)), dma((2, 4)), dma((2, 4)), dma((2, 4)),
            pltpu.SemaphoreType.REGULAR((4,)),
        ],
        compiler_params=pltpu.CompilerParams(
            collective_id=0, has_side_effects=True, vmem_limit_bytes=60 * 2**20
        ),
        cost_estimate=pl.CostEstimate(flops=11 * 10**9, bytes_accessed=2**20, transcendentals=21 * 10**6),
        name="attend",
    )(queries, cache, stretch_kv, stretch_pos)


def solution(mesh):
    return jax.shard_map(
        per_device,
        mesh=mesh,
        in_specs=(P("seq", "head"), P("seq", "head"), P(("seq", "head"), None), P()),
        out_specs=P("seq", "head"),
        check_vma=False,
    )
```

```python
import functools

import jax
import jax.numpy as jnp
from jax import lax
from jax.experimental import pallas as pl
from jax.experimental.pallas import tpu as pltpu
from jax.sharding import PartitionSpec as P

MESH = pl.DeviceIdType.MESH
F32, BF16 = jnp.float32, jnp.bfloat16
HD = 128
QD = 128
BLOCK = 512
TILE = 256
BIG = 1e30
A, B, X, Y = range(4)
KINDS = ((A, B), (X, Y), (B, X), (A, Y))
ROWS = (0, 0, 1, 2)
UNITS = (0, 4, 2, 3, 1, 6, 8, 7, 5, 10, 11, 14, 15, 18, 19, 9, 12, 13, 16, 17)
LATE = (1, 1, 1, 0, 0, 0, 1, 1, 0, 0, 1, 1, 1, 1, 1, 0, 0, 0, 0, 0)
ARRIVALS = (
    ("r0",),
    ("r1", "X0_0", "A1_0", "M_0", "r2", "r3", "A1_1", "M_1", "X0_1"),
    ("A2_0",),
    ("X1_0",),
    ("A2_1", "X1_1"),
    (),
    ("n0", "X2_0"),
    ("A3_0",),
    ("X2_1",),
    ("nX0", "A3_1"),
    (),
    ("n1", "X3_0", "n2", "X3_1"),
    ("n3", "nX1"),
    ("nX2", "nX3"),
    (),
    (),
    (),
    (),
    (),
    (),
    (),
)


def fold(x, op):
    parts = [x[8 * i : 8 * i + 8] for i in range(x.shape[0] // 8)]
    while len(parts) > 1:
        parts = [op(a, b) for a, b in zip(parts[::2], parts[1::2])]
    return parts[0]


def dot(a, b):
    return lax.dot_general(a, b, (((1,), (0,)), ((), ())), preferred_element_type=F32)


def choose(index, values):
    found = jnp.int32(values[0])
    for k, value in enumerate(values[1:], 1):
        found = jnp.where(index == k, jnp.int32(value), found)
    return found


def kernel(
    q_ref, cache_ref, new_ref, pos_ref, out_ref,
    kv, vt, qt, q_own, q_in, scores, acc, top, total, tri, bias, po, plse, so, slse,
    loc, siba_s, siba_r, sibx_s, sibx_r, y_s, y_r, z1_s, z3_s, z_r, all_s, all_r,
    nz_s, nz_r, nsa_s, nsa_r, nsx_s, nsx_r, ny_s, ny_r, q_s, q_r, o_s, o_r, l_s, l_r, met,
):
    me = lax.axis_index("seq")
    head = lax.axis_index("head")
    heads = 8
    core = me % 2
    y = (me // 2) % 4
    z = me // 8

    def seq(zz, yy, cc):
        return (zz * 4 + yy) * 2 + cc

    def at(zz, yy, cc):
        return {"seq": seq(zz, yy, cc)}

    ys = (y + 3 + 2 * core) % 4
    yr = (y + 5 - 2 * core) % 4
    z1 = z + 1 - 2 * (z % 2)
    z2 = (z + 2) % 4
    z3 = 3 - z
    other = 1 - core
    mid = jnp.logical_or(z == 1, z == 2)
    end = jnp.logical_or(z == 0, z == 3)
    to_sib, to_ys, to_yr = at(z, y, other), at(z, ys, core), at(z, yr, core)
    to_z1, to_z3 = at(z1, y, core), at(z3, y, core)

    def remote(src, dst, ss, rs, dev):
        return pltpu.make_async_remote_copy(
            src_ref=src, dst_ref=dst, send_sem=ss, recv_sem=rs, device_id=dev, device_id_type=MESH
        )

    def half(d, kind, h):
        return kv.at[4 * d + kind, pl.ds(h * 256, 256)]

    def own(h):
        return cache_ref.at[pl.ds(h * 256, 256)]

    def sib_a(d, h):
        src = half(d, A, h) if d else own(h)
        return remote(src, half(d, B, h), siba_s.at[d, h], siba_r.at[d, h], to_sib)

    def sib_x(d, h):
        return remote(half(d, X, h), half(d, Y, h), sibx_s.at[d, h], sibx_r.at[d, h], to_sib)

    def along_y(d, h):
        src = half(d, A, h) if d else own(h)
        return remote(src, half(d, X, h), y_s.at[d, h], y_r.at[d, h], to_ys)

    def outward(d, h):
        src = own(h) if d == 1 else half(5 - d, A, h)
        return remote(src, half(d, A, h), z1_s.at[d, h], z_r.at[d, h], to_z1)

    def inward(d, h):
        src = own(h) if d == 3 else half(1, A, h)
        return remote(src, half(d, A, h), z3_s.at[d, h], z_r.at[d, h], to_z3)

    def fresh(kind, d):
        return kv.at[16 + kind, pl.ds(d * QD, QD)]

    def spread(k):
        g = (head + k) % heads
        return remote(
            new_ref.at[:, pl.ds(pl.multiple_of(g * 256, 256), 256)],
            kv.at[16, pl.ds(pl.multiple_of(head * 16, 16), 16)],
            all_s.at[k], all_r.at[k], {"head": g},
        )

    def spread_in(k):
        g = (head + heads - k) % heads
        spot = kv.at[16, pl.ds(pl.multiple_of(g * 16, 16), 16)]
        return remote(spot, spot, all_s.at[k], all_r.at[k], {"head": g})

    def own_new():
        return pltpu.make_async_copy(
            new_ref.at[:, pl.ds(pl.multiple_of(head * 256, 256), 256)],
            kv.at[16, pl.ds(pl.multiple_of(head * 16, 16), 16)],
            loc.at[0],
        )

    def own_cache():
        return pltpu.make_async_copy(cache_ref, kv.at[0], loc.at[1])

    def own_queries():
        return pltpu.make_async_copy(q_ref, q_own, loc.at[2])

    def new_z(d):
        return remote(fresh(A, 0), fresh(A, d), nz_s.at[d], nz_r.at[d], {1: to_z1, 2: at(z2, y, core), 3: to_z3}[d])

    def new_y(d):
        return remote(fresh(A, d), fresh(X, d), ny_s.at[d], ny_r.at[d], to_ys)

    def new_sib_a(d):
        return remote(fresh(A, d), fresh(B, d), nsa_s.at[d], nsa_r.at[d], to_sib)

    def new_y_other(d):
        return remote(fresh(A, d), fresh(Y, d), nsx_s.at[d], nsx_r.at[d], at(z, ys, other))

    def queries(s, h):
        cols = pl.ds(h * 512, 512)
        return remote(q_ref.at[:, cols], q_in.at[s, :, cols], q_s.at[s, h], q_r.at[s, h], to_ys if s else to_yr)

    def partial(s, t):
        return remote(so.at[s, t], po.at[1 - s, t], o_s.at[s, t], o_r.at[1 - s, t], to_yr if s else to_ys)

    def partial_logs(s):
        return remote(slse.at[s], plse.at[1 - s], l_s.at[s], l_r.at[1 - s], to_yr if s else to_ys)

    own_cache().start()
    own_queries().start()
    own_new().start()
    barrier = pltpu.get_barrier_semaphore()
    x = head % 4
    height = (head // 4) * 4 + z

    def line(k):
        up = (height + 8 + k) % 8
        return {"seq": seq(up % 4, y, core), "head": (up // 4) * 4 + x}

    def greet(sem):
        @pl.when(height < 7)
        def _():
            pl.semaphore_signal(sem, inc=1, device_id=line(1), device_id_type=MESH)

        @pl.when(height > 0)
        def _():
            pl.semaphore_signal(sem, inc=1, device_id=line(-1), device_id_type=MESH)

    adjoining = jnp.where(jnp.logical_or(height == 0, height == 7), 1, 2)
    peers = [to_sib, to_ys, to_yr] + [{"head": (head // 4) * 4 + (x + k) % 4} for k in range(1, 4)]
    for peer in peers:
        pl.semaphore_signal(barrier, inc=1, device_id=peer, device_id_type=MESH)
    greet(barrier)

    key_at = lax.broadcasted_iota(jnp.int32, (QD, TILE), 0)
    row_at = lax.broadcasted_iota(jnp.int32, (QD, TILE), 1) % QD
    tri[0] = jnp.zeros((QD, TILE), F32)
    tri[1] = jnp.where(key_at <= row_at, 0.0, -BIG)
    row_pos = [pos_ref[me], pos_ref[seq(z, ys, core)], pos_ref[seq(z, yr, core)]]
    places = {A: (y, core), B: (y, other), X: (yr, core), Y: (ys, other)}
    for b in range(8):
        bias[b] = jnp.float32(0.0)
    for kind, blocks in enumerate(KINDS):
        for b in range(8):
            yy, cc = places[blocks[b // 4]]
            key_pos = pos_ref[seq((z, z1, z2, z3)[b % 4], yy, cc)]
            hidden = jnp.where(key_pos < row_pos[ROWS[kind]], 0.0, BIG).astype(F32)
            bias[(1 + kind) * 8 + b] = jnp.float32(0.0) if kind == 0 and b == 0 else hidden
    acc[...] = jnp.zeros_like(acc)
    top[...] = jnp.full_like(top, -BIG)
    total[...] = jnp.zeros_like(total)

    pl.semaphore_wait(barrier, len(peers) + adjoining)
    for h in range(2):
        outward(1, h).start()
        pl.when(mid)(lambda: inward(3, h).start())
        along_y(0, h).start()
        sib_a(0, h).start()
        for s in range(2):
            queries(s, h).start()

    greet(met.at[0])

    def place_queries(ref, rows):
        for h in range(8):
            q = ref[:, h * HD : (h + 1) * HD].astype(F32) * (HD ** -0.5 * 1.4426950408889634)
            high = q.astype(BF16)
            low = (q - high.astype(F32)).astype(BF16)
            tile, cols = rows * 4 + h // 2, pl.ds(h % 2 * HD, HD)
            qt[tile, :HD, cols] = high.T
            qt[tile, HD:, cols] = low.T

    own_queries().wait()
    place_queries(q_own, 0)
    own_cache().wait()

    def on_a(d, h):
        outward(d, h).wait_recv() if d < 3 else pl.when(end)(lambda: outward(3, h).wait_recv())
        along_y(d, h).start()
        sib_a(d, h).start()
        if d < 3:
            pl.when(mid)(lambda: (inward(2, h) if d == 1 else outward(3, h)).start())

    def on_mid(h):
        @pl.when(mid)
        def _():
            inward(3, h).wait_recv()
            outward(2, h).start()

    def on_x(d, h):
        along_y(d, h).wait_recv()
        sib_x(d, h).start()

    def on_new(d):
        if d == 0:
            own_new().wait()
            for k in range(1, heads):
                spread_in(k).wait_recv()
            for k in range(1, 4):
                new_z(k).start()
        else:
            new_z(d).wait_recv()
        new_y(d).start()
        new_y_other(d).start()
        new_sib_a(d).start()

    def on_new_x(d):
        new_y(d).wait_recv()

    def on_round(k):
        pl.semaphore_wait(met.at[k], adjoining)
        if k < 3:
            greet(met.at[k + 1])
        else:
            for g in range(1, heads):
                spread(g).start()

    def arrival(name):
        if name[0] == "A":
            on_a(int(name[1]), int(name[3]))
        elif name[0] == "M":
            on_mid(int(name[2]))
        elif name[0] == "X":
            on_x(int(name[1]), int(name[3]))
        elif name[0] == "r":
            on_round(int(name[1]))
        elif name[1] == "X":
            on_new_x(int(name[2]))
        else:
            on_new(int(name[1]))

    def prepare(block):
        d, kind = block // 4, block % 4
        if d < 4:
            waits = [] if kind in (A, X) else [(sib_a if kind == B else sib_x)(d, h) for h in range(2)]
        else:
            waits = [] if kind in (A, X) else [(new_sib_a if kind == B else new_y_other)(k) for k in range(4)]
        for w in waits:
            w.wait_recv()
        vt[block] = kv[block, :, HD:].T

    def neighbour_queries():
        for s in range(2):
            for h in range(2):
                queries(s, h).wait_recv()
            place_queries(q_in.at[s], 1 + s)

    def hand_back(s):
        logs = []
        for t in range(4):
            tile = 4 * (1 + s) + t
            weight = jnp.sum(total[tile], 0, keepdims=True)
            so[s, t] = (acc[tile] / weight).astype(BF16)
            logs.append(top[tile][:1] + jnp.log2(weight))
            partial(s, t).start()
        slse[s] = jnp.concatenate(logs + logs, 0)
        partial_logs(s).start()

    def parts(unit):
        d, kind = unit // 4, unit % 4
        first = 4 * d + choose(kind, [k[0] for k in KINDS])
        second = 4 * d + choose(kind, [k[1] for k in KINDS])
        shift = jnp.where(d == 4, 1 + kind, 0) * 8
        return (first, second), choose(kind, ROWS) * 4, shift, jnp.where(unit == 16, 1, 0)

    def piece_scores(unit, t, buf, j):
        blocks, tile, shift, diagonal = unit
        k = kv[blocks[j], :, :HD]
        s = dot(jnp.concatenate([k, k], 1), qt[tile + t])
        best = None
        for b in range(BLOCK // QD):
            part = s[b * QD : (b + 1) * QD]
            if j == 0 and b == 0:
                part = part + tri[diagonal]
            scores[buf, pl.ds(j * BLOCK + b * QD, QD), :] = part
            here = fold(part, jnp.maximum) - bias[shift + j * (BLOCK // QD) + b]
            best = here if best is None else jnp.maximum(best, here)
        return best

    def step(unit, t, buf, unit2, t2):
        blocks, tile, shift, _ = unit
        tile = tile + t
        old = top[tile]
        new = jnp.maximum(old, jnp.max(scores[buf, 2 * BLOCK :, :], 0, keepdims=True))
        shrink = jnp.exp2(old - new)
        top[tile] = new
        best = weight = value = None
        for j in range(2):
            here = piece_scores(unit2, t2, 1 - buf, j)
            best = here if best is None else jnp.maximum(best, here)
            probs = []
            for b in range(BLOCK // QD):
                edge = new[:1] + bias[shift + j * (BLOCK // QD) + b]
                p = jnp.exp2(scores[buf, pl.ds(j * BLOCK + b * QD, QD), :] - edge)
                part = fold(p, jnp.add)
                weight = part if weight is None else weight + part
                probs.append(p.astype(BF16))
            part = dot(vt[blocks[j]], jnp.concatenate(probs, 0))
            value = part if value is None else value + part
        scores[1 - buf, 2 * BLOCK :, :] = best
        total[tile] = total[tile] * shrink + weight
        acc[tile] = acc[tile] * shrink[:1] + value

    def first_scores(unit):
        unit = parts(jnp.int32(unit))
        scores[0, 2 * BLOCK :, :] = jnp.maximum(piece_scores(unit, 0, 0, 0), piece_scores(unit, 0, 0, 1))

    todo = [[functools.partial(arrival, name) for name in names] for names in ARRIVALS]
    ready, asked = set(), False
    for u, unit in enumerate(UNITS):
        d, kind = unit // 4, unit % 4
        when = u if LATE[u] else u - 1
        for block in (4 * d + KINDS[kind][0], 4 * d + KINDS[kind][1]):
            if block not in ready:
                ready.add(block)
                todo[when].append(functools.partial(prepare, block))
        if ROWS[kind] and not asked:
            asked = True
            todo[when].append(neighbour_queries)
        if LATE[u]:
            todo[u].append(functools.partial(first_scores, unit))
    for s in range(2):
        last = max(u for u, unit in enumerate(UNITS) if ROWS[unit % 4] == 1 + s)
        todo[last + 1].append(functools.partial(hand_back, s))

    def body(u, carry):
        code = choose(u, UNITS)
        ahead = choose(u, [code if late else unit for unit, late, code in zip(UNITS[1:], LATE[1:], UNITS)] + [UNITS[-1]])
        for k, actions in enumerate(todo[: len(UNITS)]):
            if actions:
                @pl.when(u == k)
                def _():
                    for action in actions:
                        action()

        unit, unit2 = parts(code), parts(ahead)
        for t in range(4):
            step(unit, t, t % 2, unit if t < 3 else unit2, (t + 1) % 4)
        return carry

    lax.fori_loop(0, len(UNITS), body, 0)
    for action in todo[len(UNITS)]:
        action()

    for s in range(2):
        partial_logs(s).wait_recv()
    for t in range(4):
        for s in range(2):
            partial(s, t).wait_recv()
        weight = jnp.sum(total[t], 0, keepdims=True)
        logs = [top[t][:1] + jnp.log2(weight), plse[0, pl.ds(t, 1)], plse[1, pl.ds(t, 1)]]
        best = jnp.maximum(logs[0], jnp.maximum(logs[1], logs[2]))
        shares = [jnp.exp2(x - best) for x in logs]
        norm = 1.0 / (shares[0] + shares[1] + shares[2])
        result = acc[t] * (shares[0] * norm / weight)
        for s in range(2):
            result = result + po[s, t].astype(F32) * (shares[1 + s] * norm)
        for h in range(2):
            out_ref[:, pl.ds((2 * t + h) * HD, HD)] = result[:, h * HD : (h + 1) * HD].T.astype(BF16)

    for k in range(1, heads):
        spread(k).wait_send()
    for h in range(2):
        for d in range(4):
            sib_a(d, h).wait_send()
            sib_x(d, h).wait_send()
            along_y(d, h).wait_send()
        outward(1, h).wait_send()
        for s in range(2):
            queries(s, h).wait_send()
    for d in range(4):
        new_sib_a(d).wait_send()
        new_y_other(d).wait_send()
        new_y(d).wait_send()
    for d in range(1, 4):
        new_z(d).wait_send()
    for s in range(2):
        partial_logs(s).wait_send()
        for t in range(4):
            partial(s, t).wait_send()

    @pl.when(mid)
    def _():
        for h in range(2):
            outward(2, h).wait_send()
            outward(3, h).wait_send()
            inward(2, h).wait_send()
            inward(3, h).wait_send()


def per_device(queries, cache, stretch_kv, stretch_pos):
    dma = pltpu.SemaphoreType.DMA
    hbm = pl.BlockSpec(memory_space=pltpu.HBM)
    return pl.pallas_call(
        kernel,
        out_shape=pltpu.VMEM(queries.shape, BF16),
        in_specs=[hbm, hbm, hbm, pl.BlockSpec(memory_space=pltpu.SMEM)],
        out_specs=pl.BlockSpec(memory_space=pltpu.VMEM),
        scratch_shapes=[
            pltpu.VMEM((20, BLOCK, 2 * HD), BF16),
            pltpu.VMEM((20, HD, BLOCK), BF16),
            pltpu.VMEM((12, 2 * HD, TILE), BF16),
            pltpu.VMEM((QD, 1024), BF16),
            pltpu.VMEM((2, QD, 1024), BF16),
            pltpu.VMEM((2, 2 * BLOCK + 8, TILE), F32),
            pltpu.VMEM((12, HD, TILE), F32),
            pltpu.VMEM((12, 8, TILE), F32),
            pltpu.VMEM((12, 8, TILE), F32),
            pltpu.VMEM((2, QD, TILE), F32),
            pltpu.SMEM((40,), F32),
            pltpu.VMEM((2, 4, HD, TILE), BF16),
            pltpu.VMEM((2, 8, TILE), F32),
            pltpu.VMEM((2, 4, HD, TILE), BF16),
            pltpu.VMEM((2, 8, TILE), F32),
            dma((3,)), dma((4, 2)), dma((4, 2)), dma((4, 2)), dma((4, 2)), dma((4, 2)), dma((4, 2)),
            dma((4, 2)), dma((4, 2)), dma((4, 2)), dma((8,)), dma((8,)),
            dma((4,)), dma((4,)), dma((4,)), dma((4,)), dma((4,)), dma((4,)), dma((4,)), dma((4,)),
            dma((2, 2)), dma((2, 2)), dma((2, 4)), dma((2, 4)), dma((2,)), dma((2,)),
            pltpu.SemaphoreType.REGULAR((4,)),
        ],
        compiler_params=pltpu.CompilerParams(
            collective_id=0, has_side_effects=True, vmem_limit_bytes=60 * 2**20
        ),
        cost_estimate=pl.CostEstimate(flops=11 * 10**9, bytes_accessed=2**20, transcendentals=21 * 10**6),
        name="attend",
    )(queries, cache, stretch_kv, stretch_pos)


def solution(mesh):
    return jax.shard_map(
        per_device,
        mesh=mesh,
        in_specs=(P("seq", "head"), P("seq", "head"), P(("seq", "head"), None), P()),
        out_specs=P("seq", "head"),
        check_vma=False,
    )
```
